32 devices in a mesh: group: 2 (over x), rows: 16 (over z, y, core).
Axes of the slice: x: 2, y: 2, z: 4, core: 2. Of those that a mesh axis runs over, the one named last changes fastest.
Arguments:
- basis: bfloat16 [131072, 1024], P(('group', 'rows')), parts along dimension 0
- thermal_load: bfloat16 [32, 131072], P(None, ('group', 'rows')), parts along dimension 1, may hold values from -3 to 3
- pressure_load: bfloat16 [32, 131072], P(None, ('group', 'rows')), parts along dimension 1, may hold values from -3 to 3
- heat_coef: bfloat16 [131072], P(('group', 'rows')), parts along dimension 0, may hold values from 0.5 to 2
- node_pad: int32 [131072], P(('group', 'rows')), parts along dimension 0, may hold values from 0 to 35, as said below
- pad_factor: float32 [72], P('group'), parts along dimension 0, may hold values from 0.3 to 3
- node_owner: int32 [65536, 1], P(('group', 'rows')), parts along dimension 0, may hold values from 0 to 15; in each aligned block of 2048 rows (0 to 2047, 2048 to 4095, ...) at most 256 rows name the same one
- node_row: int32 [65536], P(('group', 'rows')), parts along dimension 0, may hold values from 0 to 4095
- tile_count: int32 [32, 16], P(('group', 'rows')), parts along dimension 0, may hold values from 1 to 128, 1792 in all within a row
- clearance: float32 [65536], P(('group', 'rows')), parts along dimension 0, may hold values from 0.5 to 2
- speed: float32 [32], replicated, may hold values from 0.5 to 2
- mode_scale: float32 [2048], P('group'), parts along dimension 0, may hold values from 0.3 to 3
- modal_flex: bfloat16 [2048, 1024], P('group'), parts along dimension 0, may hold values from -0.1875 to 0.1875
Outputs:
- nodal_deflection: float32 [32, 131072], P(None, ('group', 'rows')), parts along dimension 1
- modal_response: float32 [64, 1024], P('group'), parts along dimension 0
- film_gap: float32 [32, 65536], P(None, ('group', 'rows')), parts along dimension 1
- nodal_press: float32 [32, 131072], P(None, ('group', 'rows')), parts along dimension 1
The draws below stay inside these ranges and needn't reach their ends.
There are 2 independent parts, one for each index of `group`. The reference program is written for one: setup_inputs(seed, part) draws one part's arguments, and reference() takes and returns one part's arrays. A program takes and returns all parts, laid end to end along the dimension named above; an argument that names none is the same for every part. Nothing has to cross between parts.
Inputs may be any that keep to these rules, and one draw needn't show every extreme that they name: `node_owner`: among the 2048 slots of one device, one row block is named at most 256 times, and that bound is reached. `tile_count`: the counts of one device's tiles sum to 1792. `node_pad`: the nodes of each pad form one run of consecutive node indices, the pads in increasing order along the nodes; every pad has nodes.
All inputs are finite; a program needn't handle non-finite values.
Results may differ from the reference program's by a relative error of at most 0.04.
Values sent between devices are 32-bit elements; how exact they have to be, the bound alone decides.
A program may use at most 64 MiB of HBM per device.

```python
import math
import jax
import jax.numpy as jnp
import numpy as np
from jax import lax

MODES = 1024
CASES = 32
PADS = 36
ROWS_DEV = 4096
TILES_DEV = 16
TILE_PTS = 128
BLOCKS = 16
NODES = 65536
S_DEV = 2048
SLOTS = 32768
CAP = 256
LIVE_DEV = 1792
LIVE = 28672


def draw_basis(key, part):
    subkeys = jax.random.split(jax.random.fold_in(key, 7), 5)
    node_ids = jnp.arange(NODES, dtype=jnp.int32)
    frequency = jax.random.randint(subkeys[0], (MODES,), 1, 17).astype(jnp.int32)
    phase_shift = jax.random.uniform(subkeys[1], (MODES,), jnp.float32, -math.pi, math.pi)
    periods = jax.random.randint(subkeys[2], (), 2, 7).astype(jnp.int32)
    row_phase = jax.random.uniform(subkeys[3], (), jnp.float32, -math.pi, math.pi)
    mode_turn = node_ids[:, None] * frequency[None, :] % NODES
    mode_wave = jnp.cos(2.0 * math.pi / NODES * mode_turn.astype(jnp.float32) + phase_shift[None, :])
    row_turn = node_ids * periods % NODES
    row_wave = jnp.sin(2.0 * math.pi / NODES * row_turn.astype(jnp.float32) + row_phase)
    rough_part = jax.random.normal(subkeys[4], (NODES, MODES), jnp.float32)
    combined = (rough_part + math.sqrt(2.0) * mode_wave) * jnp.exp(0.6 * row_wave)[:, None]
    combined = combined / (1.67 * math.sqrt(MODES))
    return combined.astype(jnp.bfloat16)


def draw_node_pad(key, part):
    spacing = NODES // PADS
    reach = spacing // 4
    offsets = jax.random.randint(jax.random.fold_in(key, 11), (PADS - 1,), -reach, reach + 1).astype(jnp.int32)
    bounds = jnp.arange(1, PADS, dtype=jnp.int32) * NODES // PADS + offsets
    node_ids = jnp.arange(NODES, dtype=jnp.int32)
    return jnp.sum((node_ids[:, None] >= bounds[None, :]).astype(jnp.int32), axis=1).astype(jnp.int32)


def with_ends(drawn, key, least, top_value):
    extent = drawn.shape
    place = [jax.random.randint(jax.random.fold_in(key, axis), (), 0, extent[axis]) for axis in range(len(extent))]
    drawn = drawn.at[tuple(place)].set(least)
    longest = extent.index(max(extent))
    place[longest] = (place[longest] + 1) % extent[longest]
    return drawn.at[tuple(place)].set(top_value)


def block_levels(own_key, shape, pieces, smallest, high):
    def one(dim, parts):
        draws = jax.random.uniform(jax.random.fold_in(jax.random.fold_in(own_key, 6), dim), (parts,), jnp.float32, smallest / len(pieces), high / len(pieces))
        return jnp.repeat(jnp.exp(draws), shape[dim] // parts).reshape((-1,) + (1,) * (len(shape) - dim - 1))

    gain = one(*pieces[0])
    for cut in pieces[1:]:
        gain = gain * one(*cut)
    return gain


def split_up(amount, total, limit, skew):
    portions = [(1 << 20) // math.isqrt(rank ** skew) + 1 for rank in range(2, amount + 1)]
    surplus, counts = total - limit - (amount - 1), [1] * (amount - 1)
    while surplus > 0:
        candidates = [i for i in range(amount - 1) if counts[i] < limit]
        pool, left = sum([portions[i] for i in candidates]), surplus
        for i in candidates:
            extra = min(limit - counts[i], max(1, left * portions[i] // pool), surplus)
            counts[i] = counts[i] + extra
            surplus = surplus - extra
    return np.array([limit] + counts)


def uneven_parts(own_key, count, total, bound, skew):
    if count == 2:
        one = jax.random.randint(own_key, (), max(1, total - bound), min(bound, total - 1) + 1)
        return jnp.stack([one, total - one])
    tallies = jnp.asarray(split_up(count, total, bound, skew), jnp.int32)
    twos = (count - 1) // 2
    source_of, sink = tallies[1:1 + 2 * twos:2], tallies[2:2 + 2 * twos:2]
    slack = jnp.minimum(source_of - 1, bound - sink)
    shifted = jax.random.randint(jax.random.fold_in(own_key, 1), (twos,), 0, 1 << 20) % (slack + 1)
    tallies = tallies.at[1:1 + 2 * twos:2].set(source_of - shifted).at[2:2 + 2 * twos:2].set(sink + shifted)
    return tallies[jax.random.permutation(jax.random.fold_in(own_key, 2), count)]


def deal_out(stream_key, own, number, rows, count, top, most, lean):
    order = jax.random.permutation(stream_key, count)
    packed, usual = load_shares(count, rows * top, most, lean, True), load_shares(count, rows * top, most, lean, False)
    places = jnp.arange(count)

    def named(sizes, turn):
        used = int((sizes > 0).sum())
        fixed = max(1, used // 4)
        moved = fixed + (places - fixed + turn * (used - fixed)) % max(1, count - fixed)
        return jnp.zeros((count,), jnp.int32).at[order[jnp.where(places < fixed, places, moved)]].set(jnp.asarray(sizes, jnp.int32))

    sizes = jnp.where(number % 4 == 0, named(packed, number // 4), named(usual, number - number // 4 - 1))
    mixed = jax.random.permutation(jax.random.fold_in(own, 3), count)
    giver, taker = mixed[0:count // 2 * 2:2], mixed[1:count // 2 * 2:2]
    slack = jnp.minimum(sizes[giver] - 1, most - sizes[taker]) // 2
    slack = jnp.where((giver == order[0]) | (taker == order[0]) | (sizes[taker] == 0), 0, jnp.maximum(slack, 0))
    moved = jax.random.randint(jax.random.fold_in(own, 4), (count // 2,), 0, 1 << 20) % (slack + 1)
    sizes = sizes.at[giver].add(-moved).at[taker].add(moved)
    items = jnp.searchsorted(jnp.cumsum(sizes), jnp.arange(rows * top), side="right").astype(jnp.int32)
    table = items.reshape(top, rows).T
    table = table[jax.random.permutation(jax.random.fold_in(own, 1), rows)]
    turn = jax.random.randint(jax.random.fold_in(own, 2), (rows, 1), 0, top)
    return jnp.take_along_axis(table, (jnp.arange(top)[None, :] + turn) % top, axis=1)


def load_shares(count, total, limit, skew, full):
    loads = [(1 << 20) // math.isqrt(standing ** skew) + 1 for standing in range(1, count + 1)]
    largest = limit if full else min(limit, max(-(-total // count), total * loads[0] // sum(loads)))
    least = 1 if total - largest >= count - 1 else 0
    given, spare = [largest] + [least] * (count - 1), total - largest - least * (count - 1)
    while spare > 0:
        movable = [i for i in range(1, count) if given[i] < largest] or [i for i in range(1, count) if given[i] < limit]
        mass, budget = sum([loads[i] for i in movable]), spare
        for i in movable:
            extra = min(limit - given[i], max(1, budget * loads[i] // mass), spare)
            given[i] = given[i] + extra
            spare = spare - extra
    return np.array(given)


def scatter_about(key, extent, width, most, pieces=(), held_as=jnp.bfloat16):
    gain = block_levels(key, extent, pieces, -0.22, 0.18) if pieces else 1.0
    array = jax.random.normal(key, extent, jnp.float32) * width * gain
    return jnp.minimum(jnp.maximum(array, -most), most).astype(held_as)


def setup_inputs(seed: int = 0, part: int = 0) -> dict:
    key_of = jax.random.split(jax.random.key(seed), 14)
    own_keys = jax.random.split(jax.random.fold_in(key_of[13], part), 14)
    basis = draw_basis(jax.random.fold_in(jax.random.fold_in(key_of[13], part), 71), part)
    thermal_load = scatter_about(own_keys[1], (CASES, NODES), 0.5, 3.0, ((1, 16),))
    pressure_load = scatter_about(own_keys[2], (CASES, NODES), 0.5, 3.0, ((1, 16),))
    heat_coef = jnp.clip(jnp.exp(math.log(2.0) - 1.3862944 * jax.random.uniform(own_keys[3], (NODES,), jnp.float32) ** block_levels(own_keys[3], (NODES,), ((0, 16),), -0.2, 0.2)), 0.5, 2.0).astype(jnp.bfloat16)
    node_pad = draw_node_pad(jax.random.fold_in(jax.random.fold_in(key_of[13], part), 71), part)
    pad_factor = jnp.clip(jnp.exp(jax.random.uniform(own_keys[5], (PADS,), jnp.float32, math.log(0.3), math.log(3.0))), 0.3, 3.0)
    node_owner_keys = jax.random.split(jax.random.fold_in(own_keys[6], 1), SLOTS // S_DEV)
    node_owner_turns = jax.random.permutation(jax.random.fold_in(own_keys[6], 3), SLOTS // S_DEV)
    node_owner = jax.vmap(lambda own, number: deal_out(jax.random.fold_in(own_keys[6], 2), own, number, S_DEV, BLOCKS, 1, CAP, 2))(node_owner_keys, node_owner_turns).reshape((SLOTS, 1))
    node_row = with_ends(jax.random.randint(own_keys[7], (SLOTS,), 0, ROWS_DEV), jax.random.fold_in(own_keys[7], 1), 0, ROWS_DEV - 1).astype(jnp.int32)
    tile_count = jax.vmap(lambda own: uneven_parts(own, TILES_DEV, LIVE_DEV, TILE_PTS, 1))(jax.random.split(own_keys[8], BLOCKS)).reshape((BLOCKS, TILES_DEV)).astype(jnp.int32)
    clearance = jnp.clip(jnp.exp(math.log(2.0) - 1.3862944 * jax.random.uniform(own_keys[9], (SLOTS,), jnp.float32) ** block_levels(own_keys[9], (SLOTS,), ((0, 16),), -0.2, 0.2)), 0.5, 2.0)
    speed = jnp.clip(jnp.exp(jax.random.uniform(key_of[10], (CASES,), jnp.float32, math.log(0.5), math.log(2.0))), 0.5, 2.0)
    mode_scale = jnp.clip(jnp.exp(jax.random.uniform(own_keys[11], (MODES,), jnp.float32, math.log(0.3), math.log(3.0))), 0.3, 3.0)
    modal_flex = scatter_about(own_keys[12], (MODES, MODES), MODES ** -0.5, 0.1875)
    return dict(basis=basis, thermal_load=thermal_load, pressure_load=pressure_load, heat_coef=heat_coef, node_pad=node_pad, pad_factor=pad_factor, node_owner=node_owner, node_row=node_row, tile_count=tile_count, clearance=clearance, speed=speed, mode_scale=mode_scale, modal_flex=modal_flex)


def modal_solve(forcing, mode_scale, modal_flex):
    coupled = jnp.dot(forcing.astype(jnp.bfloat16), modal_flex, preferred_element_type=jnp.float32)
    return mode_scale[None, :] * (forcing + coupled)

def rebuild(response, basis):
    return lax.dot_general(response.astype(jnp.bfloat16), basis, (((1,), (1,)), ((), ())), preferred_element_type=jnp.float32)

def reference(basis, thermal_load, pressure_load, heat_coef, node_pad, pad_factor, node_owner, node_row, tile_count, clearance, speed, mode_scale, modal_flex):
    proj_scale = math.sqrt(MODES / NODES)
    counts_rep = jnp.repeat(tile_count.reshape(-1), TILE_PTS, total_repeat_length=SLOTS)
    live_slot = jnp.arange(SLOTS, dtype=jnp.int32) % TILE_PTS < counts_rep
    node_index = (node_owner[:, 0] * ROWS_DEV + node_row).astype(jnp.int32)
    load_one = (thermal_load.astype(jnp.float32) + pressure_load.astype(jnp.float32)).astype(jnp.bfloat16)
    modal_one = proj_scale * jnp.dot(load_one, basis, preferred_element_type=jnp.float32)
    resp_one = modal_solve(modal_one, mode_scale, modal_flex)
    field_one = rebuild(resp_one, basis)
    defl_one = jnp.where(live_slot[None, :], field_one[:, node_index], 0.0)
    film_gap_one = clearance[None, :] * jnp.exp(jnp.tanh(0.25 * defl_one))
    film_press = jnp.where(live_slot[None, :], speed[:, None] / (film_gap_one * film_gap_one), 0.0)
    nodal_press = jnp.zeros((CASES, NODES), jnp.float32).at[:, node_index].add(film_press)
    pad_total = jax.ops.segment_sum(nodal_press.T, node_pad, PADS).T
    pad_heat = pad_total * pad_factor[None, :] * (PADS / LIVE)
    pad_mask = node_pad[None, :] == jnp.arange(PADS, dtype=jnp.int32)[:, None]
    weighted = jnp.where(pad_mask, heat_coef[None, :], jnp.zeros((), jnp.bfloat16)).astype(jnp.bfloat16)
    heat_basis = proj_scale * jnp.dot(weighted, basis, preferred_element_type=jnp.float32)
    press_modal = proj_scale * jnp.dot(nodal_press.astype(jnp.bfloat16), basis, preferred_element_type=jnp.float32)
    modal_two = modal_one + press_modal + jnp.dot(pad_heat, heat_basis, precision=lax.Precision.HIGHEST)
    modal_response = modal_solve(modal_two, mode_scale, modal_flex)
    nodal_deflection = rebuild(modal_response, basis)
    defl_two = nodal_deflection[:, node_index]
    film_gap = jnp.where(live_slot[None, :], clearance[None, :] * jnp.exp(jnp.tanh(0.25 * defl_two)), 0.0)
    return (nodal_deflection, modal_response, film_gap, nodal_press)
```

```python
import functools
import math

import jax
import jax.numpy as jnp
from jax import lax
from jax.experimental import pallas as pl
from jax.experimental.pallas import tpu as pltpu
from jax.sharding import PartitionSpec as P

LIVE_DEV = 1792
LANES = 128
F32 = jnp.float32
BF16 = jnp.bfloat16
NT = (((1,), (1,)), ((), ()))


def dot(a, b):
    return jnp.dot(a, b, preferred_element_type=F32)


def dot_nt(a, b):
    return lax.dot_general(a, b, NT, preferred_element_type=F32)


def kernel(
    n,
    own,
    basis_h,
    thermal,
    pressure,
    heat_coef,
    node_pad,
    pad_factor,
    owner,
    row,
    live,
    clear,
    speed,
    mode_scale,
    flex_h,
    defl_o,
    resp_o,
    gap_o,
    press_o,
    basis,
    flex,
    xs,
    padm,
    wp,
    rw,
    wl,
    qs,
    rq,
    rank,
    s1,
    r1,
    g1,
    hb,
    rh,
    s2,
    r2,
    g2,
    fs,
    rf,
    acc,
    bsem,
    ssem,
    rsem,
):
    me = lax.axis_index("rows")
    cases, modes = resp_o.shape
    nodes = basis.shape[0]
    slots = row.shape[1]
    pads_r = rh.shape[1]
    piece = s1.shape[1]
    capp = rq.shape[2]
    his = nodes // LANES
    chunks = bsem.shape[0] - 1
    rows_c = nodes // chunks
    proj_scale = math.sqrt(modes / (nodes * n))
    per_row = cases // piece

    for i in range(chunks):
        part = pl.ds(i * rows_c, rows_c)
        pltpu.make_async_copy(basis_h.at[part], basis.at[part], bsem.at[i]).start()
    flex_copy = pltpu.make_async_copy(flex_h, flex, bsem.at[chunks])
    flex_copy.start()

    barrier = pltpu.get_barrier_semaphore()

    def greet(k, c):
        pl.semaphore_signal(barrier, inc=1, device_id={"rows": lax.rem(me + k, n)})
        return c

    lax.fori_loop(1, n, greet, 0)

    def remote(phase, k, src, dst, peer):
        return pltpu.make_async_remote_copy(
            src_ref=src,
            dst_ref=dst,
            send_sem=ssem.at[phase, k],
            recv_sem=rsem.at[phase, k],
            device_id={"rows": peer},
        )

    def each(body):
        def step(k, c):
            body(k, lax.rem(me + k, n), lax.rem(me + n - k, n))
            return c

        lax.fori_loop(1, n, step, 0)

    def only(cond, body):
        if own == n:
            body()
        else:
            pl.when(cond)(body)

    ids = owner[...]
    rows = row[...]
    row_hi = lax.shift_right_logical(rows, 7)
    row_lo = rows & (LANES - 1)
    step_c = 256
    strict = (
        lax.broadcasted_iota(jnp.int32, (step_c, step_c), 0)
        < lax.broadcasted_iota(jnp.int32, (step_c, step_c), 1)
    ).astype(BF16)
    oh_o = (lax.broadcasted_iota(jnp.int32, (n, slots), 0) == ids).astype(F32)
    carry = jnp.zeros((n, 1), F32)
    for b in range(slots // step_c):
        part = oh_o[:, b * step_c : (b + 1) * step_c]
        before = dot(part.astype(BF16), strict) + carry
        carry = carry + jnp.sum(part, axis=1, keepdims=True)
        rank[:, b * step_c : (b + 1) * step_c] = jnp.sum(
            part * before, axis=0, keepdims=True
        ).astype(jnp.int32)
    oh_p = (lax.broadcasted_iota(jnp.int32, (capp, slots), 0) == rank[...]).astype(F32).astype(BF16)
    asked = dot_nt((oh_o * row_hi.astype(F32)).astype(BF16), oh_p) * float(LANES) + dot_nt(
        (oh_o * row_lo.astype(F32)).astype(BF16), oh_p
    )
    asked = asked.astype(jnp.int32)
    for o in range(n):
        qs[o] = asked[o : o + 1, :]

    inv = 1.0 / clear[...]
    weight = live[...] * inv * inv
    w_hi = weight.astype(BF16).astype(F32)
    w_lo = weight - w_hi
    lo_hit = lax.broadcasted_iota(jnp.int32, (LANES, slots), 0) == row_lo
    b_w = jnp.concatenate(
        [jnp.where(lo_hit, w_hi, 0.0).astype(BF16), jnp.where(lo_hit, w_lo, 0.0).astype(BF16)], axis=0
    )
    node_hi = ids * his + row_hi
    for o in range(0, n, 16):
        rows_o = 16 * his
        a_w = (
            (lax.broadcasted_iota(jnp.int32, (rows_o, slots), 0) + o * his == node_hi)
            .astype(F32)
            .astype(BF16)
        )
        both = dot_nt(a_w, b_w)
        wp[o : o + 16] = (both[:, :LANES] + both[:, LANES:]).reshape(16, his, LANES)

    xs[0:cases, :] = (thermal[...].astype(F32) + pressure[...].astype(F32)).astype(BF16)
    pad_ids = lax.broadcasted_iota(jnp.int32, (padm.shape[0], nodes), 0)
    hit = pad_ids == node_pad[...]
    padm[...] = hit.astype(F32).astype(BF16)
    xs[cases:, :] = jnp.where(
        hit[: xs.shape[0] - cases], heat_coef[...].astype(F32), 0.0
    ).astype(BF16)
    for i in range(chunks):
        part = pl.ds(i * rows_c, rows_c)
        pltpu.make_async_copy(basis_h.at[part], basis.at[part], bsem.at[i]).wait()
        got = dot(xs[:, i * rows_c : (i + 1) * rows_c], basis[part, :])
        if i == 0:
            acc[...] = got
        else:
            acc[...] += got
    for j in range(own):
        blk, r0 = j // per_row, (j % per_row) * piece
        s1[j] = proj_scale * acc[r0 : r0 + piece, blk * LANES : (blk + 1) * LANES]
    for m in range(modes // LANES):
        hb[m] = proj_scale * acc[cases : cases + pads_r, m * LANES : (m + 1) * LANES]

    pl.semaphore_wait(barrier, n - 1)

    def first_copy(k, peer):
        return remote(0, k, s1.at[peer], r1.at[k], peer)

    each(lambda k, to, fr: only(to < own, lambda: first_copy(k, to).start()))

    def weight_copy(k, peer):
        return remote(1, k, wp.at[peer], rw.at[k], peer)

    def ask_copy(k, peer):
        return remote(2, k, qs.at[peer], rq.at[k], peer)

    def heat_copy(k, peer):
        return remote(3, k, hb.at[lax.div(peer, per_row)], rh.at[k], peer)

    rq[0] = qs[me]

    def reduce_first():
        each(lambda k, to, fr: first_copy(k, to).wait_recv())
        g1[me] = s1[me] + functools.reduce(lambda a, b: a + b, [r1[k] for k in range(1, n)])

    only(me < own, reduce_first)

    def share_copy(phase, g, k, peer):
        return remote(phase, k, g.at[me], g.at[me], peer)

    def share_wait(phase, g, k, fr):
        remote(phase, k, g.at[fr], g.at[fr], fr).wait_recv()

    only(me < own, lambda: each(lambda k, to, fr: share_copy(4, g1, k, to).start()))
    each(lambda k, to, fr: weight_copy(k, to).start())
    each(lambda k, to, fr: ask_copy(k, to).start())
    each(lambda k, to, fr: only(to < own, lambda: heat_copy(k, to).start()))
    each(lambda k, to, fr: only(fr < own, lambda: share_wait(4, g1, k, fr)))

    def gathered(g):
        flat = g[...].reshape(own * piece, LANES)
        return jnp.concatenate(
            [flat[m * cases : (m + 1) * cases] for m in range(modes // LANES)], axis=1
        )

    def solve(forcing):
        return mode_scale[...] * (forcing + dot(forcing.astype(BF16), flex[...]))

    flex_copy.wait()
    resp = solve(gathered(g1)).astype(BF16)

    each(lambda k, to, fr: weight_copy(k, to).wait_recv())
    wl[...] = wp[me] + functools.reduce(lambda a, b: a + b, [rw[k] for k in range(1, n)])
    pad_part = jnp.zeros((cases, padm.shape[0]), F32)
    for i in range(chunks):
        lo, hi = i * rows_c, (i + 1) * rows_c
        field = dot_nt(resp, basis[lo:hi, :])
        w_row = jnp.concatenate(
            [wl[h : h + 1, :] for h in range(lo // LANES, hi // LANES)], axis=1
        )
        press = speed[...] * jnp.exp(-2.0 * jnp.tanh(0.25 * field)) * w_row
        press_o[:, lo:hi] = press
        press = press.astype(BF16)
        got = dot(press, basis[lo:hi, :])
        if i == 0:
            acc[0:cases, :] = got
        else:
            acc[0:cases, :] += got
        pad_part = pad_part + dot_nt(press, padm[:, lo:hi])
    for j in range(own):
        blk, r0 = j // per_row, (j % per_row) * piece
        s2[j, 0:piece] = proj_scale * acc[r0 : r0 + piece, blk * LANES : (blk + 1) * LANES]
        s2[j, piece:] = pad_part[r0 : r0 + piece, :]

    def second_copy(k, peer):
        return remote(5, k, s2.at[peer], r2.at[k], peer)

    each(lambda k, to, fr: only(to < own, lambda: second_copy(k, to).start()))

    def reduce_second():
        each(lambda k, to, fr: heat_copy(k, to).wait_recv())
        heat = hb[lax.div(me, per_row)] + functools.reduce(
            lambda a, b: a + b, [rh[k] for k in range(1, n)]
        )
        heat = jnp.concatenate([heat, jnp.zeros((LANES - pads_r, LANES), F32)], axis=0)
        each(lambda k, to, fr: second_copy(k, to).wait_recv())
        total = s2[me] + functools.reduce(lambda a, b: a + b, [r2[k] for k in range(1, n)])
        pad_heat = total[piece:] * pad_factor[...]
        g2[me] = (
            g1[me]
            + total[:piece]
            + jnp.dot(pad_heat, heat, precision=lax.Precision.HIGHEST, preferred_element_type=F32)
        )

    only(me < own, reduce_second)
    only(me < own, lambda: each(lambda k, to, fr: share_copy(6, g2, k, to).start()))
    each(lambda k, to, fr: only(fr < own, lambda: share_wait(6, g2, k, fr)))
    resp2 = solve(gathered(g2))
    resp_o[...] = resp2
    resp2 = resp2.astype(BF16)
    for i in range(chunks):
        lo, hi = i * rows_c, (i + 1) * rows_c
        defl_o[:, lo:hi] = dot_nt(resp2, basis[lo:hi, :])

    each(lambda k, to, fr: ask_copy(k, to).wait_recv())

    def pick(k):
        out = []
        for c in range(capp // LANES):
            idx = jnp.broadcast_to(rq[k][:, c * LANES : (c + 1) * LANES], (cases, LANES))
            idx_hi = lax.shift_right_logical(idx, 7)
            idx_lo = idx & (LANES - 1)
            val = jnp.zeros((cases, LANES), F32)
            for h in range(his):
                got = jnp.take_along_axis(defl_o[:, h * LANES : (h + 1) * LANES], idx_lo, axis=1)
                val = jnp.where(idx_hi == h, got, val)
            out.append(val)
        return jnp.concatenate(out, axis=1) if len(out) > 1 else out[0]

    def answer_copy(k, peer):
        return remote(7, k, fs.at[k], rf.at[me], peer)

    def answer(k, to, fr):
        fs[k] = pick(k)
        answer_copy(k, fr).start()

    each(answer)
    rf[me] = pick(0)
    each(lambda k, to, fr: remote(7, k, fs.at[k], rf.at[to], to).wait_recv())

    def place(t, c):
        part = pl.ds(pl.multiple_of(t * LANES, LANES), LANES)
        own_t = jnp.broadcast_to(owner[:, part], (cases, LANES))
        pos_t = jnp.broadcast_to(rank[:, part], (cases, LANES))
        blk = own_t * (capp // LANES) + lax.shift_right_logical(pos_t, 7)
        lane = pos_t & (LANES - 1)
        val = jnp.zeros((cases, LANES), F32)
        for o in range(n):
            for s in range(capp // LANES):
                got = jnp.take_along_axis(rf[o, :, s * LANES : (s + 1) * LANES], lane, axis=1)
                val = jnp.where(blk == o * (capp // LANES) + s, got, val)
        gap_o[:, part] = live[:, part] * clear[:, part] * jnp.exp(jnp.tanh(0.25 * val))
        return c

    lax.fori_loop(0, slots // LANES, place, 0)

    def drain(k, to, fr):
        def owned():
            first_copy(k, to).wait_send()
            heat_copy(k, to).wait_send()
            second_copy(k, to).wait_send()

        def mine():
            share_copy(4, g1, k, to).wait_send()
            share_copy(6, g2, k, to).wait_send()

        weight_copy(k, to).wait_send()
        ask_copy(k, to).wait_send()
        answer_copy(k, fr).wait_send()
        only(to < own, owned)
        only(me < own, mine)

    each(drain)


def on_device(
    basis,
    thermal_load,
    pressure_load,
    heat_coef,
    node_pad,
    pad_factor,
    node_owner,
    node_row,
    tile_count,
    clearance,
    speed,
    mode_scale,
    modal_flex,
):
    n = lax.axis_size("rows")
    nodes, modes = basis.shape
    cases = thermal_load.shape[0]
    slots = node_row.shape[0]
    capacity = 2 * slots // n
    capp = max(LANES, -(-capacity // LANES) * LANES)
    tiles = tile_count.shape[1]
    tile_pts = slots // tiles
    pads = pad_factor.shape[0]
    pads_r = -(-pads // 8) * 8
    pads_x = -(-pads // 16) * 16
    all_tiles = cases * modes // LANES
    own = min(n, all_tiles // 8)
    piece = all_tiles // own
    his = nodes // LANES
    chunks = 8

    live = (
        (jnp.arange(tile_pts, dtype=jnp.int32)[None, :] < tile_count[0][:, None])
        .astype(F32)
        .reshape(1, slots)
    )
    factor = jnp.zeros((1, LANES), F32).at[0, :pads].set(pad_factor * (pads / (LIVE_DEV * n)))

    vmem = pl.BlockSpec(memory_space=pltpu.VMEM)
    anyw = pl.BlockSpec(memory_space=pl.ANY)
    return pl.pallas_call(
        functools.partial(kernel, n, own),
        out_shape=(
            jax.ShapeDtypeStruct((cases, nodes), F32),
            jax.ShapeDtypeStruct((cases, modes), F32),
            jax.ShapeDtypeStruct((cases, slots), F32),
            jax.ShapeDtypeStruct((cases, nodes), F32),
        ),
        in_specs=[anyw] + [vmem] * 11 + [anyw],
        out_specs=(vmem,) * 4,
        scratch_shapes=[
            pltpu.VMEM((nodes, modes), BF16),
            pltpu.VMEM((modes, modes), BF16),
            pltpu.VMEM((cases + pads_x, nodes), BF16),
            pltpu.VMEM((LANES, nodes), BF16),
            pltpu.VMEM((n, his, LANES), F32),
            pltpu.VMEM((n, his, LANES), F32),
            pltpu.VMEM((his, LANES), F32),
            pltpu.VMEM((n, 1, capp), jnp.int32),
            pltpu.VMEM((n, 1, capp), jnp.int32),
            pltpu.VMEM((1, slots), jnp.int32),
            pltpu.VMEM((own, piece, LANES), F32),
            pltpu.VMEM((n, piece, LANES), F32),
            pltpu.VMEM((own, piece, LANES), F32),
            pltpu.VMEM((modes // LANES, pads_r, LANES), F32),
            pltpu.VMEM((n, pads_r, LANES), F32),
            pltpu.VMEM((own, 2 * piece, LANES), F32),
            pltpu.VMEM((n, 2 * piece, LANES), F32),
            pltpu.VMEM((own, piece, LANES), F32),
            pltpu.VMEM((n, cases, capp), F32),
            pltpu.VMEM((n, cases, capp), F32),
            pltpu.VMEM((cases + pads_x, modes), F32),
            pltpu.SemaphoreType.DMA((chunks + 1,)),
            pltpu.SemaphoreType.DMA((8, n)),
            pltpu.SemaphoreType.DMA((8, n)),
        ],
        compiler_params=pltpu.CompilerParams(
            collective_id=0, has_side_effects=True, vmem_limit_bytes=56 * 1024 * 1024
        ),
    )(
        basis,
        thermal_load,
        pressure_load,
        heat_coef.reshape(1, nodes),
        node_pad.reshape(1, nodes),
        factor,
        node_owner.reshape(1, slots),
        node_row.reshape(1, slots),
        live,
        clearance.reshape(1, slots),
        speed.reshape(cases, 1),
        mode_scale.reshape(1, modes),
        modal_flex,
    )


def solution(mesh):
    return jax.shard_map(
        on_device,
        mesh=mesh,
        in_specs=(
            P(("group", "rows"), None),
            P(None, ("group", "rows")),
            P(None, ("group", "rows")),
            P(("group", "rows")),
            P(("group", "rows")),
            P("group"),
            P(("group", "rows"), None),
            P(("group", "rows")),
            P(("group", "rows"), None),
            P(("group", "rows")),
            P(),
            P("group"),
            P("group", None),
        ),
        out_specs=(
            P(None, ("group", "rows")),
            P("group", None),
            P(None, ("group", "rows")),
            P(None, ("group", "rows")),
        ),
        check_vma=False,
    )
```

```python
import functools
import math

import jax
import jax.numpy as jnp
from jax import lax
from jax.experimental import pallas as pl
from jax.experimental.pallas import tpu as pltpu
from jax.sharding import PartitionSpec as P

LIVE_DEV = 1792
LANES = 128
F32 = jnp.float32
BF16 = jnp.bfloat16
NT = (((1,), (1,)), ((), ()))


def dot(a, b):
    return jnp.dot(a, b, preferred_element_type=F32)


def dot_nt(a, b):
    return lax.dot_general(a, b, NT, preferred_element_type=F32)


def kernel(
    n,
    own,
    basis_h,
    thermal,
    pressure,
    heat_coef,
    node_pad,
    pad_factor,
    owner,
    row,
    tile_count,
    clear,
    speed,
    mode_scale,
    flex_h,
    defl_h,
    resp_h,
    gap_h,
    press_h,
    defl_o,
    resp_o,
    gap_o,
    press_o,
    basis,
    flex,
    xs,
    padm,
    live,
    wl,
    qs,
    rq,
    rank,
    s1,
    r1,
    g1,
    hb,
    rh,
    hfull,
    s2,
    r2,
    g2,
    fs,
    rf,
    acc,
    bsem,
    osem,
    ssem,
    rsem,
):
    me = lax.axis_index("rows")
    cases, modes = resp_o.shape
    nodes = basis.shape[0]
    slots = row.shape[1]
    rows_h = rh.shape[1]
    pads_r = xs.shape[0] - cases
    piece = s1.shape[1]
    capp = rq.shape[2]
    his = nodes // LANES
    chunks = bsem.shape[0] - 1
    rows_c = nodes // chunks
    proj_scale = math.sqrt(modes / (nodes * n))
    per_row = cases // piece
    packed = s2.shape[1] - piece < piece
    half = LANES // 2

    for i in range(chunks):
        part = pl.ds(i * rows_c, rows_c)
        pltpu.make_async_copy(basis_h.at[part], basis.at[part], bsem.at[i]).start()
    flex_copy = pltpu.make_async_copy(flex_h, flex, bsem.at[chunks])
    flex_copy.start()

    barrier = pltpu.get_barrier_semaphore()

    def greet(k, c):
        pl.semaphore_signal(barrier, inc=1, device_id={"rows": lax.rem(me + k, n)})
        return c

    lax.fori_loop(1, n, greet, 0)

    def remote(phase, k, src, dst, peer):
        return pltpu.make_async_remote_copy(
            src_ref=src,
            dst_ref=dst,
            send_sem=ssem.at[phase, k],
            recv_sem=rsem.at[phase, k],
            device_id={"rows": peer},
        )

    def each(body):
        def step(i, c):
            k = n // 2 + lax.div(i, 2) * (1 - 2 * lax.rem(i, 2))
            body(k, lax.rem(me + k, n), lax.rem(me + n - k, n))
            return c

        lax.fori_loop(1, n, step, 0)

    def only(cond, body):
        if own == n:
            body()
        else:
            pl.when(cond)(body)

    ids = owner[...]
    rows = row[...]
    row_hi = lax.shift_right_logical(rows, 7)
    row_lo = rows & (LANES - 1)
    step_c = 256
    strict = (
        lax.broadcasted_iota(jnp.int32, (step_c, step_c), 0)
        < lax.broadcasted_iota(jnp.int32, (step_c, step_c), 1)
    ).astype(BF16)
    oh_o = (lax.broadcasted_iota(jnp.int32, (n, slots), 0) == ids).astype(F32)
    carry = jnp.zeros((n, 1), F32)
    for b in range(slots // step_c):
        part = oh_o[:, b * step_c : (b + 1) * step_c]
        before = dot(part.astype(BF16), strict) + carry
        carry = carry + jnp.sum(part, axis=1, keepdims=True)
        rank[:, b * step_c : (b + 1) * step_c] = jnp.sum(
            part * before, axis=0, keepdims=True
        ).astype(jnp.int32)
    oh_p = (lax.broadcasted_iota(jnp.int32, (capp, slots), 0) == rank[...]).astype(F32).astype(BF16)
    tiles = tile_count.shape[1]
    lane_id = lax.broadcasted_iota(jnp.int32, (1, slots), 1)
    spread = lax.div(lax.broadcasted_iota(jnp.int32, (tiles, slots), 1), slots // tiles)
    spread = (spread == lax.broadcasted_iota(jnp.int32, (tiles, slots), 0)).astype(F32).astype(BF16)
    counts = jnp.broadcast_to(tile_count[...].astype(F32), (8, tiles)).astype(BF16)
    counts = dot(counts, spread)[0:1, :]
    live[...] = (lax.rem(lane_id, slots // tiles).astype(F32) < counts).astype(F32)
    inv = 1.0 / clear[...]
    weight = live[...] * inv * inv
    w_hi = weight.astype(BF16).astype(F32)
    parts = (row_hi.astype(F32), row_lo.astype(F32), w_hi, weight - w_hi)
    asked = dot_nt(jnp.concatenate([(oh_o * v).astype(BF16) for v in parts], axis=0), oh_p)
    asked_row = asked[0:n] * float(LANES) + asked[n : 2 * n]
    asked_w = asked[2 * n : 3 * n] + asked[3 * n :]
    for o in range(n):
        qs[o, 0:1] = asked_row[o : o + 1, :]
        qs[o, 1:2] = asked_w[o : o + 1, :]

    def ask_copy(k, peer):
        return remote(2, k, qs.at[peer], rq.at[k], peer)

    pl.semaphore_wait(barrier, n - 1)
    each(lambda k, to, fr: ask_copy(k, to).start())
    rq[0] = qs[me]

    xs[0:cases, :] = (thermal[...].astype(F32) + pressure[...].astype(F32)).astype(BF16)
    pad_ids = lax.broadcasted_iota(jnp.int32, (padm.shape[0], nodes), 0)
    hit = (pad_ids & (half - 1)) == node_pad[...]
    coef = heat_coef[...].astype(F32)
    coef = jnp.concatenate([coef[h : h + 1, :] for h in range(his)], axis=1)
    padm[...] = hit.astype(F32).astype(BF16)
    xs[cases:, :] = jnp.where(hit[:pads_r], coef, 0.0).astype(BF16)
    for i in range(chunks):
        part = pl.ds(i * rows_c, rows_c)
        pltpu.make_async_copy(basis_h.at[part], basis.at[part], bsem.at[i]).wait()
        got = dot(xs[:, i * rows_c : (i + 1) * rows_c], basis[part, :])
        if i == 0:
            acc[...] = got
        else:
            acc[...] += got
    for j in range(own):
        blk, r0 = j // per_row, (j % per_row) * piece
        s1[j] = proj_scale * acc[r0 : r0 + piece, blk * LANES : (blk + 1) * LANES]
        h0 = cases + (j % per_row) * rows_h
        hb[j] = proj_scale * acc[h0 : h0 + rows_h, blk * LANES : (blk + 1) * LANES]

    def first_copy(k, peer):
        return remote(0, k, s1.at[peer], r1.at[k], peer)

    each(lambda k, to, fr: only(to < own, lambda: first_copy(k, to).start()))

    def heat_copy(k, peer):
        return remote(3, k, hb.at[peer], rh.at[k], peer)

    def reduce_first():
        each(lambda k, to, fr: first_copy(k, to).wait_recv())
        g1[me] = s1[me] + functools.reduce(lambda a, b: a + b, [r1[k] for k in range(1, n)])

    only(me < own, reduce_first)

    def share_copy(phase, g, k, peer):
        return remote(phase, k, g.at[me], g.at[me], peer)

    def share_wait(phase, g, k, fr):
        remote(phase, k, g.at[fr], g.at[fr], fr).wait_recv()

    only(me < own, lambda: each(lambda k, to, fr: share_copy(4, g1, k, to).start()))
    each(lambda k, to, fr: only(to < own, lambda: heat_copy(k, to).start()))
    each(lambda k, to, fr: ask_copy(k, to).wait_recv())
    both = jnp.zeros((his, 2 * LANES), F32)
    for k in range(n):
        idx = rq[k, 0:1].astype(jnp.int32)
        wgt = rq[k, 1:2]
        top = wgt.astype(BF16).astype(F32)
        hi_hit = lax.broadcasted_iota(jnp.int32, (his, capp), 0) == lax.shift_right_logical(idx, 7)
        lo_hit = lax.broadcasted_iota(jnp.int32, (LANES, capp), 0) == (idx & (LANES - 1))
        b_w = jnp.concatenate(
            [jnp.where(lo_hit, top, 0.0), jnp.where(lo_hit, wgt - top, 0.0)], axis=0
        ).astype(BF16)
        both = both + dot_nt(hi_hit.astype(F32).astype(BF16), b_w)
    wl[...] = both[:, :LANES] + both[:, LANES:]
    eye = lax.broadcasted_iota(jnp.int32, (cases, cases), 0) == lax.broadcasted_iota(
        jnp.int32, (cases, cases), 1
    )
    speed_c = jnp.sum(jnp.where(eye, speed[...], 0.0), axis=1, keepdims=True)
    each(lambda k, to, fr: only(fr < own, lambda: share_wait(4, g1, k, fr)))

    def gathered(g):
        flat = g[...].reshape(own * piece, LANES)
        return jnp.concatenate(
            [flat[m * cases : (m + 1) * cases] for m in range(modes // LANES)], axis=1
        )

    def solve(forcing):
        return mode_scale[...] * (forcing + dot(forcing.astype(BF16), flex[...]))

    flex_copy.wait()
    resp = solve(gathered(g1)).astype(BF16)

    pad_part = jnp.zeros((cases, padm.shape[0]), F32)
    for i in range(chunks):
        lo, hi = i * rows_c, (i + 1) * rows_c
        field = dot_nt(resp, basis[lo:hi, :])
        w_row = jnp.concatenate(
            [wl[h : h + 1, :] for h in range(lo // LANES, hi // LANES)], axis=1
        )
        press = speed_c * jnp.exp(-2.0 * jnp.tanh(0.25 * field)) * w_row
        press_o[:, lo:hi] = press
        press = press.astype(BF16)
        got = dot(press, basis[lo:hi, :])
        if i == 0:
            acc[0:cases, :] = got
        else:
            acc[0:cases, :] += got
        pad_part = pad_part + dot_nt(press, padm[:, lo:hi])
    low = lax.broadcasted_iota(jnp.int32, (cases, LANES), 1) < half
    for j in range(own):
        blk, r0 = j // per_row, (j % per_row) * piece
        s2[j, 0:piece] = proj_scale * acc[r0 : r0 + piece, blk * LANES : (blk + 1) * LANES]
        if packed:
            mid = r0 + piece // 2
            s2[j, piece:] = jnp.where(low[r0:mid], pad_part[r0:mid], pad_part[mid : r0 + piece])
        else:
            s2[j, piece:] = pad_part[r0 : r0 + piece, :]

    def out_copy(i, src, dst):
        return pltpu.make_async_copy(src, dst, osem.at[i])

    def second_copy(k, peer):
        return remote(5, k, s2.at[peer], r2.at[k], peer)

    each(lambda k, to, fr: only(to < own, lambda: second_copy(k, to).start()))

    out_copy(0, press_o, press_h).start()
    mine_h = lax.rem(me, per_row)

    def mate_copy(d):
        mate = me - mine_h + lax.rem(mine_h + d, per_row)
        return pltpu.make_async_remote_copy(
            src_ref=hfull.at[mine_h],
            dst_ref=hfull.at[mine_h],
            send_sem=ssem.at[1, d],
            recv_sem=rsem.at[1, d],
            device_id={"rows": mate},
        )

    def mate_wait(d):
        other = lax.rem(mine_h + per_row - d, per_row)
        pltpu.make_async_remote_copy(
            src_ref=hfull.at[other],
            dst_ref=hfull.at[other],
            send_sem=ssem.at[1, d],
            recv_sem=rsem.at[1, d],
            device_id={"rows": me - mine_h + other},
        ).wait_recv()

    def reduce_second():
        each(lambda k, to, fr: heat_copy(k, to).wait_recv())
        hfull[mine_h] = hb[me] + functools.reduce(
            lambda a, b: a + b, [rh[k] for k in range(1, n)]
        )
        for d in range(1, per_row):
            mate_copy(d).start()
        fac = jnp.concatenate(
            [pad_factor[...], jnp.zeros((1, half - pad_factor.shape[1]), F32)], axis=1
        )
        fac = jnp.concatenate([fac, fac], axis=1) * (pad_factor.shape[1] / (LIVE_DEV * n))
        for d in range(1, per_row):
            mate_wait(d)
        heat = hfull[...].reshape(pads_r, LANES)
        if pads_r < half:
            heat = jnp.concatenate([heat, jnp.zeros((half - pads_r, LANES), F32)], axis=0)
        heat = jnp.concatenate([heat, heat], axis=0)
        each(lambda k, to, fr: second_copy(k, to).wait_recv())
        total = s2[me] + functools.reduce(lambda a, b: a + b, [r2[k] for k in range(1, n)])
        pad_heat = total[piece:] * fac
        left = low[: pad_heat.shape[0]]
        rows_l = jnp.where(left, pad_heat, 0.0)
        if packed:
            rows_l = jnp.concatenate([rows_l, jnp.where(left, 0.0, pad_heat)], axis=0)
        g2[me] = (
            g1[me]
            + total[:piece]
            + jnp.dot(rows_l, heat, precision=lax.Precision.HIGHEST, preferred_element_type=F32)
        )

    only(me < own, reduce_second)
    only(me < own, lambda: each(lambda k, to, fr: share_copy(6, g2, k, to).start()))
    each(lambda k, to, fr: only(fr < own, lambda: share_wait(6, g2, k, fr)))
    resp2 = solve(gathered(g2))
    resp_o[...] = resp2
    out_copy(1, resp_o, resp_h).start()
    resp2 = resp2.astype(BF16)
    for i in range(chunks):
        lo, hi = i * rows_c, (i + 1) * rows_c
        defl_o[:, lo:hi] = dot_nt(resp2, basis[lo:hi, :])

    out_copy(2, defl_o, defl_h).start()


    def pick(k):
        out = []
        for c in range(capp // LANES):
            idx = jnp.broadcast_to(rq[k, 0:1, c * LANES : (c + 1) * LANES].astype(jnp.int32), (cases, LANES))
            idx_hi = lax.shift_right_logical(idx, 7)
            idx_lo = idx & (LANES - 1)
            val = jnp.zeros((cases, LANES), F32)
            for h in range(his):
                got = jnp.take_along_axis(defl_o[:, h * LANES : (h + 1) * LANES], idx_lo, axis=1)
                val = jnp.where(idx_hi == h, got, val)
            out.append(val)
        return jnp.concatenate(out, axis=1) if len(out) > 1 else out[0]

    def answer_copy(k, peer):
        return remote(7, k, fs.at[k], rf.at[me], peer)

    def answer(k, to, fr):
        fs[k] = pick(k)
        answer_copy(k, fr).start()

    each(answer)
    rf[me] = pick(0)
    each(lambda k, to, fr: remote(7, k, fs.at[k], rf.at[to], to).wait_recv())

    def place(t, c):
        part = pl.ds(pl.multiple_of(t * LANES, LANES), LANES)
        own_t = jnp.broadcast_to(owner[:, part], (cases, LANES))
        pos_t = jnp.broadcast_to(rank[:, part], (cases, LANES))
        blk = own_t * (capp // LANES) + lax.shift_right_logical(pos_t, 7)
        lane = pos_t & (LANES - 1)
        val = jnp.zeros((cases, LANES), F32)
        for o in range(n):
            for s in range(capp // LANES):
                got = jnp.take_along_axis(rf[o, :, s * LANES : (s + 1) * LANES], lane, axis=1)
                val = jnp.where(blk == o * (capp // LANES) + s, got, val)
        gap_o[:, part] = live[:, part] * clear[:, part] * jnp.exp(jnp.tanh(0.25 * val))
        return c

    lax.fori_loop(0, slots // LANES, place, 0)
    out_copy(3, gap_o, gap_h).start()

    def drain(k, to, fr):
        def owned():
            first_copy(k, to).wait_send()
            heat_copy(k, to).wait_send()
            second_copy(k, to).wait_send()

        def mine():
            share_copy(4, g1, k, to).wait_send()
            share_copy(6, g2, k, to).wait_send()

        ask_copy(k, to).wait_send()
        answer_copy(k, fr).wait_send()
        only(to < own, owned)
        only(me < own, mine)

    each(drain)
    for d in range(1, per_row):
        only(me < own, lambda: mate_copy(d).wait_send())
    out_copy(0, press_o, press_h).wait()
    out_copy(1, resp_o, resp_h).wait()
    out_copy(2, defl_o, defl_h).wait()
    out_copy(3, gap_o, gap_h).wait()


def hand_over(*refs):
    half = (len(refs) - 1) // 2
    sems = refs[-1]
    copies = []
    for i in range(half):
        src, dst = refs[i], refs[half + i]
        for r in range(0, src.shape[0], 8):
            part = pl.ds(r, 8)
            copies.append(
                pltpu.make_async_copy(src.at[part], dst.at[part], sems.at[i, r // 8])
            )
    for c in copies:
        c.start()
    for c in copies:
        c.wait()


def on_device(
    basis,
    thermal_load,
    pressure_load,
    heat_coef,
    node_pad,
    pad_factor,
    node_owner,
    node_row,
    tile_count,
    clearance,
    speed,
    mode_scale,
    modal_flex,
):
    n = lax.axis_size("rows")
    nodes, modes = basis.shape
    cases = thermal_load.shape[0]
    slots = node_row.shape[0]
    capacity = 2 * slots // n
    capp = max(LANES, -(-capacity // LANES) * LANES)
    tiles = tile_count.shape[1]
    tile_pts = slots // tiles
    pads = pad_factor.shape[0]
    all_tiles = cases * modes // LANES
    own = min(n, all_tiles // 8)
    piece = all_tiles // own
    per_row = cases // piece
    rows_h = -(-pads // (8 * per_row)) * 8
    pads_r = rows_h * per_row
    extra = piece // 2 if piece % 16 == 0 else piece
    his = nodes // LANES
    chunks = 8

    vmem = pl.BlockSpec(memory_space=pltpu.VMEM)
    anyw = pl.BlockSpec(memory_space=pl.ANY)
    outs = pl.pallas_call(
        functools.partial(kernel, n, own),
        out_shape=(
            jax.ShapeDtypeStruct((cases, nodes), F32),
            jax.ShapeDtypeStruct((cases, modes), F32),
            jax.ShapeDtypeStruct((cases, slots), F32),
            jax.ShapeDtypeStruct((cases, nodes), F32),
        ),
        in_specs=[anyw] + [vmem] * 11 + [anyw],
        out_specs=(anyw,) * 4,
        scratch_shapes=[
            pltpu.VMEM((cases, nodes), F32),
            pltpu.VMEM((cases, modes), F32),
            pltpu.VMEM((cases, slots), F32),
            pltpu.VMEM((cases, nodes), F32),
            pltpu.VMEM((nodes, modes), BF16),
            pltpu.VMEM((modes, modes), BF16),
            pltpu.VMEM((cases + pads_r, nodes), BF16),
            pltpu.VMEM((LANES, nodes), BF16),
            pltpu.VMEM((1, slots), F32),
            pltpu.VMEM((his, LANES), F32),
            pltpu.VMEM((n, 2, capp), F32),
            pltpu.VMEM((n, 2, capp), F32),
            pltpu.VMEM((1, slots), jnp.int32),
            pltpu.VMEM((own, piece, LANES), F32),
            pltpu.VMEM((n, piece, LANES), F32),
            pltpu.VMEM((own, piece, LANES), F32),
            pltpu.VMEM((own, rows_h, LANES), F32),
            pltpu.VMEM((n, rows_h, LANES), F32),
            pltpu.VMEM((per_row, rows_h, LANES), F32),
            pltpu.VMEM((own, piece + extra, LANES), F32),
            pltpu.VMEM((n, piece + extra, LANES), F32),
            pltpu.VMEM((own, piece, LANES), F32),
            pltpu.VMEM((n, cases, capp), F32),
            pltpu.VMEM((n, cases, capp), F32),
            pltpu.VMEM((cases + pads_r, modes), F32),
            pltpu.SemaphoreType.DMA((chunks + 1,)),
            pltpu.SemaphoreType.DMA((4,)),
            pltpu.SemaphoreType.DMA((8, n)),
            pltpu.SemaphoreType.DMA((8, n)),
        ],
        compiler_params=pltpu.CompilerParams(
            collective_id=0, has_side_effects=True, vmem_limit_bytes=56 * 1024 * 1024
        ),
    )(
        basis,
        thermal_load,
        pressure_load,
        heat_coef.reshape(his, LANES),
        node_pad.reshape(1, nodes),
        pad_factor.reshape(1, pads),
        node_owner.reshape(1, slots),
        node_row.reshape(1, slots),
        tile_count,
        clearance.reshape(1, slots),
        speed.reshape(1, cases),
        mode_scale.reshape(1, modes),
        modal_flex,
    )
    return pl.pallas_call(
        hand_over,
        out_shape=tuple(jax.ShapeDtypeStruct(o.shape, o.dtype) for o in outs),
        in_specs=[anyw] * 4,
        out_specs=(anyw,) * 4,
        scratch_shapes=[pltpu.SemaphoreType.DMA((4, cases // 8))],
    )(*outs)


def solution(mesh):
    return jax.shard_map(
        on_device,
        mesh=mesh,
        in_specs=(
            P(("group", "rows"), None),
            P(None, ("group", "rows")),
            P(None, ("group", "rows")),
            P(("group", "rows")),
            P(("group", "rows")),
            P("group"),
            P(("group", "rows"), None),
            P(("group", "rows")),
            P(("group", "rows"), None),
            P(("group", "rows")),
            P(),
            P("group"),
            P("group", None),
        ),
        out_specs=(
            P(None, ("group", "rows")),
            P("group", None),
            P(None, ("group", "rows")),
            P(None, ("group", "rows")),
        ),
        check_vma=False,
    )
```

```python
import functools
import math

import jax
import jax.numpy as jnp
from jax import lax
from jax.experimental import pallas as pl
from jax.experimental.pallas import tpu as pltpu
from jax.sharding import PartitionSpec as P

LIVE_DEV = 1792
LANES = 128
F32 = jnp.float32
BF16 = jnp.bfloat16
NT = (((1,), (1,)), ((), ()))


def dot(a, b):
    return jnp.dot(a, b, preferred_element_type=F32)


def dot_nt(a, b):
    return lax.dot_general(a, b, NT, preferred_element_type=F32)


def kernel(
    n,
    own,
    basis_h,
    thermal,
    pressure,
    heat_coef,
    node_pad,
    pad_factor,
    owner,
    row,
    tile_count,
    clear,
    speed,
    mode_scale,
    flex_h,
    defl_h,
    resp_h,
    gap_h,
    press_h,
    defl_o,
    resp_o,
    gap_o,
    press_o,
    basis,
    flex,
    xs,
    padm,
    live,
    wl,
    qs,
    rq,
    rank,
    s1,
    r1,
    g1,
    hb,
    rh,
    hfull,
    s2,
    r2,
    g2,
    fs,
    rf,
    acc,
    bsem,
    osem,
    ssem,
    rsem,
):
    me = lax.axis_index("rows")
    cases, modes = resp_o.shape
    nodes = basis.shape[0]
    slots = row.shape[1]
    rows_h = rh.shape[1]
    pads_r = xs.shape[0] - cases
    piece = s1.shape[1]
    capp = rq.shape[2]
    his = nodes // LANES
    chunks = bsem.shape[0] - 1
    rows_c = nodes // chunks
    proj_scale = math.sqrt(modes / (nodes * n))
    per_row = cases // piece
    packed = s2.shape[1] - piece < piece
    half = LANES // 2

    for i in range(chunks):
        part = pl.ds(i * rows_c, rows_c)
        pltpu.make_async_copy(basis_h.at[part], basis.at[part], bsem.at[i]).start()
    flex_copy = pltpu.make_async_copy(flex_h, flex, bsem.at[chunks])
    flex_copy.start()

    barrier = pltpu.get_barrier_semaphore()

    def greet(k, c):
        pl.semaphore_signal(barrier, inc=1, device_id={"rows": lax.rem(me + k, n)})
        return c

    lax.fori_loop(1, n, greet, 0)

    def remote(phase, k, src, dst, peer):
        return pltpu.make_async_remote_copy(
            src_ref=src,
            dst_ref=dst,
            send_sem=ssem.at[phase, k],
            recv_sem=rsem.at[phase, k],
            device_id={"rows": peer},
        )

    def each(body):
        def step(i, c):
            k = n // 2 + lax.div(i, 2) * (1 - 2 * lax.rem(i, 2))
            body(k, lax.rem(me + k, n), lax.rem(me + n - k, n))
            return c

        lax.fori_loop(1, n, step, 0)

    def only(cond, body):
        if own == n:
            body()
        else:
            pl.when(cond)(body)

    ids = owner[...]
    rows = row[...]
    row_hi = lax.shift_right_logical(rows, 7)
    row_lo = rows & (LANES - 1)
    step_c = 256
    strict = (
        lax.broadcasted_iota(jnp.int32, (step_c, step_c), 0)
        < lax.broadcasted_iota(jnp.int32, (step_c, step_c), 1)
    ).astype(BF16)
    oh_o = (lax.broadcasted_iota(jnp.int32, (n, slots), 0) == ids).astype(F32)
    carry = jnp.zeros((n, 1), F32)
    for b in range(slots // step_c):
        part = oh_o[:, b * step_c : (b + 1) * step_c]
        before = dot(part.astype(BF16), strict) + carry
        carry = carry + jnp.sum(part, axis=1, keepdims=True)
        rank[:, b * step_c : (b + 1) * step_c] = jnp.sum(
            part * before, axis=0, keepdims=True
        ).astype(jnp.int32)
    oh_p = (lax.broadcasted_iota(jnp.int32, (capp, slots), 0) == rank[...]).astype(F32).astype(BF16)
    tiles = tile_count.shape[1]
    lane_id = lax.broadcasted_iota(jnp.int32, (1, slots), 1)
    spread = lax.div(lax.broadcasted_iota(jnp.int32, (tiles, slots), 1), slots // tiles)
    spread = (spread == lax.broadcasted_iota(jnp.int32, (tiles, slots), 0)).astype(F32).astype(BF16)
    counts = jnp.broadcast_to(tile_count[...].astype(F32), (8, tiles)).astype(BF16)
    counts = dot(counts, spread)[0:1, :]
    live[...] = (lax.rem(lane_id, slots // tiles).astype(F32) < counts).astype(F32)
    inv = 1.0 / clear[...]
    weight = live[...] * inv * inv
    w_hi = weight.astype(BF16).astype(F32)
    parts = (row_hi.astype(F32), row_lo.astype(F32), w_hi, weight - w_hi)
    asked = dot_nt(jnp.concatenate([(oh_o * v).astype(BF16) for v in parts], axis=0), oh_p)
    asked_row = asked[0:n] * float(LANES) + asked[n : 2 * n]
    asked_w = asked[2 * n : 3 * n] + asked[3 * n :]
    for o in range(n):
        qs[o, 0:1] = asked_row[o : o + 1, :]
        qs[o, 1:2] = asked_w[o : o + 1, :]

    def ask_copy(k, peer):
        return remote(2, k, qs.at[peer], rq.at[k], peer)

    pl.semaphore_wait(barrier, n - 1)
    each(lambda k, to, fr: ask_copy(k, to).start())
    rq[0] = qs[me]

    xs[0:cases, :] = (thermal[...].astype(F32) + pressure[...].astype(F32)).astype(BF16)
    pad_ids = lax.broadcasted_iota(jnp.int32, (padm.shape[0], nodes), 0)
    hit = (pad_ids & (half - 1)) == node_pad[...]
    coef = heat_coef[...].astype(F32)
    coef = jnp.concatenate([coef[h : h + 1, :] for h in range(his)], axis=1)
    padm[...] = hit.astype(F32).astype(BF16)
    xs[cases:, :] = jnp.where(hit[:pads_r], coef, 0.0).astype(BF16)
    for i in range(chunks):
        part = pl.ds(i * rows_c, rows_c)
        pltpu.make_async_copy(basis_h.at[part], basis.at[part], bsem.at[i]).wait()
        got = dot(xs[:, i * rows_c : (i + 1) * rows_c], basis[part, :])
        if i == 0:
            acc[...] = got
        else:
            acc[...] += got
    for j in range(own):
        blk, r0 = j // per_row, (j % per_row) * piece
        s1[j] = proj_scale * acc[r0 : r0 + piece, blk * LANES : (blk + 1) * LANES]
        h0 = cases + (j % per_row) * rows_h
        hb[j] = proj_scale * acc[h0 : h0 + rows_h, blk * LANES : (blk + 1) * LANES]

    def first_copy(k, peer):
        return remote(0, k, s1.at[peer], r1.at[k], peer)

    each(lambda k, to, fr: only(to < own, lambda: first_copy(k, to).start()))

    def heat_copy(k, peer):
        return remote(3, k, hb.at[peer], rh.at[k], peer)

    def reduce_first():
        each(lambda k, to, fr: first_copy(k, to).wait_recv())
        g1[me] = s1[me] + functools.reduce(lambda a, b: a + b, [r1[k] for k in range(1, n)])

    only(me < own, reduce_first)

    def share_copy(phase, g, k, peer):
        return remote(phase, k, g.at[me], g.at[me], peer)

    def share_wait(phase, g, k, fr):
        remote(phase, k, g.at[fr], g.at[fr], fr).wait_recv()

    only(me < own, lambda: each(lambda k, to, fr: share_copy(4, g1, k, to).start()))
    each(lambda k, to, fr: only(to < own, lambda: heat_copy(k, to).start()))
    each(lambda k, to, fr: ask_copy(k, to).wait_recv())
    both = jnp.zeros((his, 2 * LANES), F32)
    for k in range(n):
        idx = rq[k, 0:1].astype(jnp.int32)
        wgt = rq[k, 1:2]
        top = wgt.astype(BF16).astype(F32)
        hi_hit = lax.broadcasted_iota(jnp.int32, (his, capp), 0) == lax.shift_right_logical(idx, 7)
        lo_hit = lax.broadcasted_iota(jnp.int32, (LANES, capp), 0) == (idx & (LANES - 1))
        b_w = jnp.concatenate(
            [jnp.where(lo_hit, top, 0.0), jnp.where(lo_hit, wgt - top, 0.0)], axis=0
        ).astype(BF16)
        both = both + dot_nt(hi_hit.astype(F32).astype(BF16), b_w)
    wl[...] = both[:, :LANES] + both[:, LANES:]
    eye = lax.broadcasted_iota(jnp.int32, (cases, cases), 0) == lax.broadcasted_iota(
        jnp.int32, (cases, cases), 1
    )
    speed_c = jnp.sum(jnp.where(eye, speed[...], 0.0), axis=1, keepdims=True)
    each(lambda k, to, fr: only(fr < own, lambda: share_wait(4, g1, k, fr)))

    def gathered(g):
        flat = g[...].reshape(own * piece, LANES)
        return jnp.concatenate(
            [flat[m * cases : (m + 1) * cases] for m in range(modes // LANES)], axis=1
        )

    def solve(forcing):
        return mode_scale[...] * (forcing + dot(forcing.astype(BF16), flex[...]))

    flex_copy.wait()
    resp = solve(gathered(g1)).astype(BF16)

    pad_part = jnp.zeros((cases, padm.shape[0]), F32)
    for i in range(chunks):
        lo, hi = i * rows_c, (i + 1) * rows_c
        field = dot_nt(resp, basis[lo:hi, :])
        w_row = jnp.concatenate(
            [wl[h : h + 1, :] for h in range(lo // LANES, hi // LANES)], axis=1
        )
        press = speed_c * jnp.exp(-2.0 * jnp.tanh(0.25 * field)) * w_row
        press_o[:, lo:hi] = press
        press = press.astype(BF16)
        got = dot(press, basis[lo:hi, :])
        if i == 0:
            acc[0:cases, :] = got
        else:
            acc[0:cases, :] += got
        pad_part = pad_part + dot_nt(press, padm[:, lo:hi])
    low = lax.broadcasted_iota(jnp.int32, (cases, LANES), 1) < half
    for j in range(own):
        blk, r0 = j // per_row, (j % per_row) * piece
        s2[j, 0:piece] = proj_scale * acc[r0 : r0 + piece, blk * LANES : (blk + 1) * LANES]
        if packed:
            mid = r0 + piece // 2
            s2[j, piece:] = jnp.where(low[r0:mid], pad_part[r0:mid], pad_part[mid : r0 + piece])
        else:
            s2[j, piece:] = pad_part[r0 : r0 + piece, :]

    def out_copy(i, src, dst):
        return pltpu.make_async_copy(src, dst, osem.at[i])

    def second_copy(k, peer):
        return remote(5, k, s2.at[peer], r2.at[k], peer)

    each(lambda k, to, fr: only(to < own, lambda: second_copy(k, to).start()))

    out_copy(0, press_o, press_h).start()
    mine_h = lax.rem(me, per_row)

    def mate_copy(d):
        mate = me - mine_h + lax.rem(mine_h + d, per_row)
        return pltpu.make_async_remote_copy(
            src_ref=hfull.at[mine_h],
            dst_ref=hfull.at[mine_h],
            send_sem=ssem.at[1, d],
            recv_sem=rsem.at[1, d],
            device_id={"rows": mate},
        )

    def mate_wait(d):
        other = lax.rem(mine_h + per_row - d, per_row)
        pltpu.make_async_remote_copy(
            src_ref=hfull.at[other],
            dst_ref=hfull.at[other],
            send_sem=ssem.at[1, d],
            recv_sem=rsem.at[1, d],
            device_id={"rows": me - mine_h + other},
        ).wait_recv()

    def reduce_second():
        each(lambda k, to, fr: heat_copy(k, to).wait_recv())
        hfull[mine_h] = hb[me] + functools.reduce(
            lambda a, b: a + b, [rh[k] for k in range(1, n)]
        )
        for d in range(1, per_row):
            mate_copy(d).start()
        fac = jnp.concatenate(
            [pad_factor[...], jnp.zeros((1, half - pad_factor.shape[1]), F32)], axis=1
        )
        fac = jnp.concatenate([fac, fac], axis=1) * (pad_factor.shape[1] / (LIVE_DEV * n))
        for d in range(1, per_row):
            mate_wait(d)
        heat = hfull[...].reshape(pads_r, LANES)
        if pads_r < half:
            heat = jnp.concatenate([heat, jnp.zeros((half - pads_r, LANES), F32)], axis=0)
        heat = jnp.concatenate([heat, heat], axis=0)
        each(lambda k, to, fr: second_copy(k, to).wait_recv())
        total = s2[me] + functools.reduce(lambda a, b: a + b, [r2[k] for k in range(1, n)])
        pad_heat = total[piece:] * fac
        left = low[: pad_heat.shape[0]]
        rows_l = jnp.where(left, pad_heat, 0.0)
        if packed:
            rows_l = jnp.concatenate([rows_l, jnp.where(left, 0.0, pad_heat)], axis=0)
        g2[me] = (
            g1[me]
            + total[:piece]
            + jnp.dot(rows_l, heat, precision=lax.Precision.HIGHEST, preferred_element_type=F32)
        )

    only(me < own, reduce_second)
    only(me < own, lambda: each(lambda k, to, fr: share_copy(6, g2, k, to).start()))
    each(lambda k, to, fr: only(fr < own, lambda: share_wait(6, g2, k, fr)))
    resp2 = solve(gathered(g2))
    resp_o[...] = resp2
    out_copy(1, resp_o, resp_h).start()
    resp2 = resp2.astype(BF16)
    for i in range(chunks):
        lo, hi = i * rows_c, (i + 1) * rows_c
        defl_o[:, lo:hi] = dot_nt(resp2, basis[lo:hi, :])

    out_copy(2, defl_o, defl_h).start()


    def pick(k):
        out = []
        for c in range(capp // LANES):
            idx = jnp.broadcast_to(rq[k, 0:1, c * LANES : (c + 1) * LANES].astype(jnp.int32), (cases, LANES))
            idx_hi = lax.shift_right_logical(idx, 7)
            idx_lo = idx & (LANES - 1)
            val = jnp.zeros((cases, LANES), F32)
            for h in range(his):
                got = jnp.take_along_axis(defl_o[:, h * LANES : (h + 1) * LANES], idx_lo, axis=1)
                val = jnp.where(idx_hi == h, got, val)
            out.append(val)
        return jnp.concatenate(out, axis=1) if len(out) > 1 else out[0]

    def answer_copy(k, peer):
        return remote(7, k, fs.at[k], rf.at[me], peer)

    def answer(k, to, fr):
        fs[k] = pick(k)
        answer_copy(k, fr).start()

    each(answer)
    rf[me] = pick(0)
    blocks = capp // LANES

    def place(source, last):
        def tile(t, c):
            part = pl.ds(pl.multiple_of(t * LANES, LANES), LANES)
            own_t = jnp.broadcast_to(owner[:, part], (cases, LANES))
            pos_t = jnp.broadcast_to(rank[:, part], (cases, LANES))
            blk = (own_t - source) * blocks + lax.shift_right_logical(pos_t, 7)
            lane = pos_t & (LANES - 1)
            val = jnp.zeros((cases, LANES), F32) if last is None else gap_o[:, part]
            for s in range(blocks):
                got = jnp.take_along_axis(rf[source, :, s * LANES : (s + 1) * LANES], lane, axis=1)
                val = jnp.where(blk == s, got, val)
            gap_o[:, part] = val
            return c

        lax.fori_loop(0, slots // LANES, tile, 0)

    def receive(k, to, fr):
        remote(7, k, fs.at[k], rf.at[to], to).wait_recv()
        place(to, k)

    place(me, None)
    each(receive)
    gap_o[...] = live[...] * clear[...] * jnp.exp(jnp.tanh(0.25 * gap_o[...]))
    out_copy(3, gap_o, gap_h).start()

    def drain(k, to, fr):
        def owned():
            first_copy(k, to).wait_send()
            heat_copy(k, to).wait_send()
            second_copy(k, to).wait_send()

        def mine():
            share_copy(4, g1, k, to).wait_send()
            share_copy(6, g2, k, to).wait_send()

        ask_copy(k, to).wait_send()
        answer_copy(k, fr).wait_send()
        only(to < own, owned)
        only(me < own, mine)

    each(drain)
    for d in range(1, per_row):
        only(me < own, lambda: mate_copy(d).wait_send())
    out_copy(0, press_o, press_h).wait()
    out_copy(1, resp_o, resp_h).wait()
    out_copy(2, defl_o, defl_h).wait()
    out_copy(3, gap_o, gap_h).wait()


def hand_over(*refs):
    count = (len(refs) - 1) // 3
    sems = refs[-1]
    ins, outs, held = (refs[i * count : (i + 1) * count] for i in range(3))
    order = (3, 1, 0, 2)
    first = [pltpu.make_async_copy(ins[i], held[i], sems.at[0, i]) for i in order]
    second = [pltpu.make_async_copy(held[i], outs[i], sems.at[1, i]) for i in order]
    for c in first:
        c.start()
    for c, d in zip(first, second):
        c.wait()
        d.start()
    for d in second:
        d.wait()


def on_device(
    basis,
    thermal_load,
    pressure_load,
    heat_coef,
    node_pad,
    pad_factor,
    node_owner,
    node_row,
    tile_count,
    clearance,
    speed,
    mode_scale,
    modal_flex,
):
    n = lax.axis_size("rows")
    nodes, modes = basis.shape
    cases = thermal_load.shape[0]
    slots = node_row.shape[0]
    capacity = 2 * slots // n
    capp = max(LANES, -(-capacity // LANES) * LANES)
    tiles = tile_count.shape[1]
    tile_pts = slots // tiles
    pads = pad_factor.shape[0]
    all_tiles = cases * modes // LANES
    own = min(n, all_tiles // 8)
    piece = all_tiles // own
    per_row = cases // piece
    rows_h = -(-pads // (8 * per_row)) * 8
    pads_r = rows_h * per_row
    extra = piece // 2 if piece % 16 == 0 else piece
    his = nodes // LANES
    chunks = 8

    vmem = pl.BlockSpec(memory_space=pltpu.VMEM)
    anyw = pl.BlockSpec(memory_space=pl.ANY)
    outs = pl.pallas_call(
        functools.partial(kernel, n, own),
        out_shape=(
            jax.ShapeDtypeStruct((cases, nodes), F32),
            jax.ShapeDtypeStruct((cases, modes), F32),
            jax.ShapeDtypeStruct((cases, slots), F32),
            jax.ShapeDtypeStruct((cases, nodes), F32),
        ),
        in_specs=[anyw] + [vmem] * 11 + [anyw],
        out_specs=(anyw,) * 4,
        scratch_shapes=[
            pltpu.VMEM((cases, nodes), F32),
            pltpu.VMEM((cases, modes), F32),
            pltpu.VMEM((cases, slots), F32),
            pltpu.VMEM((cases, nodes), F32),
            pltpu.VMEM((nodes, modes), BF16),
            pltpu.VMEM((modes, modes), BF16),
            pltpu.VMEM((cases + pads_r, nodes), BF16),
            pltpu.VMEM((LANES, nodes), BF16),
            pltpu.VMEM((1, slots), F32),
            pltpu.VMEM((his, LANES), F32),
            pltpu.VMEM((n, 2, capp), F32),
            pltpu.VMEM((n, 2, capp), F32),
            pltpu.VMEM((1, slots), jnp.int32),
            pltpu.VMEM((own, piece, LANES), F32),
            pltpu.VMEM((n, piece, LANES), F32),
            pltpu.VMEM((own, piece, LANES), F32),
            pltpu.VMEM((own, rows_h, LANES), F32),
            pltpu.VMEM((n, rows_h, LANES), F32),
            pltpu.VMEM((per_row, rows_h, LANES), F32),
            pltpu.VMEM((own, piece + extra, LANES), F32),
            pltpu.VMEM((n, piece + extra, LANES), F32),
            pltpu.VMEM((own, piece, LANES), F32),
            pltpu.VMEM((n, cases, capp), F32),
            pltpu.VMEM((n, cases, capp), F32),
            pltpu.VMEM((cases + pads_r, modes), F32),
            pltpu.SemaphoreType.DMA((chunks + 1,)),
            pltpu.SemaphoreType.DMA((4,)),
            pltpu.SemaphoreType.DMA((8, n)),
            pltpu.SemaphoreType.DMA((8, n)),
        ],
        compiler_params=pltpu.CompilerParams(
            collective_id=0, has_side_effects=True, vmem_limit_bytes=56 * 1024 * 1024
        ),
    )(
        basis,
        thermal_load,
        pressure_load,
        heat_coef.reshape(his, LANES),
        node_pad.reshape(1, nodes),
        pad_factor.reshape(1, pads),
        node_owner.reshape(1, slots),
        node_row.reshape(1, slots),
        tile_count,
        clearance.reshape(1, slots),
        speed.reshape(1, cases),
        mode_scale.reshape(1, modes),
        modal_flex,
    )
    return pl.pallas_call(
        hand_over,
        out_shape=tuple(jax.ShapeDtypeStruct(o.shape, o.dtype) for o in outs),
        in_specs=[anyw] * 4,
        out_specs=(anyw,) * 4,
        scratch_shapes=[pltpu.VMEM(o.shape, o.dtype) for o in outs] + [pltpu.SemaphoreType.DMA((2, 4))],
        compiler_params=pltpu.CompilerParams(vmem_limit_bytes=8 * 1024 * 1024),
    )(*outs)


def solution(mesh):
    return jax.shard_map(
        on_device,
        mesh=mesh,
        in_specs=(
            P(("group", "rows"), None),
            P(None, ("group", "rows")),
            P(None, ("group", "rows")),
            P(("group", "rows")),
            P(("group", "rows")),
            P("group"),
            P(("group", "rows"), None),
            P(("group", "rows")),
            P(("group", "rows"), None),
            P(("group", "rows")),
            P(),
            P("group"),
            P("group", None),
        ),
        out_specs=(
            P(None, ("group", "rows")),
            P("group", None),
            P(None, ("group", "rows")),
            P(None, ("group", "rows")),
        ),
        check_vma=False,
    )
```

```python
import functools
import math

import jax
import jax.numpy as jnp
from jax import lax
from jax.experimental import pallas as pl
from jax.experimental.pallas import tpu as pltpu
from jax.sharding import PartitionSpec as P

LIVE_DEV = 1792
LANES = 128
F32 = jnp.float32
BF16 = jnp.bfloat16
NT = (((1,), (1,)), ((), ()))


def dot(a, b):
    return jnp.dot(a, b, preferred_element_type=F32)


def dot_nt(a, b):
    return lax.dot_general(a, b, NT, preferred_element_type=F32)


def kernel(
    n,
    own,
    basis_h,
    thermal,
    pressure,
    heat_coef,
    node_pad,
    pad_factor,
    owner,
    row,
    tile_count,
    clear,
    speed,
    mode_scale,
    flex_h,
    defl_h,
    resp_h,
    gap_h,
    press_h,
    defl_o,
    resp_o,
    gap_o,
    press_o,
    basis,
    flex,
    xs,
    padm,
    live,
    wl,
    qs,
    rq,
    rank,
    s1,
    r1,
    g1,
    hb,
    rh,
    hfull,
    s2,
    r2,
    g2,
    fs,
    rf,
    acc,
    bsem,
    osem,
    ssem,
    rsem,
):
    me = lax.axis_index("rows")
    cases, modes = resp_o.shape
    nodes = basis.shape[0]
    slots = row.shape[1]
    rows_h = rh.shape[1]
    pads_r = xs.shape[0] - cases
    piece = s1.shape[1]
    capp = rq.shape[2]
    his = nodes // LANES
    chunks = bsem.shape[0] - 1
    rows_c = nodes // chunks
    proj_scale = math.sqrt(modes / (nodes * n))
    per_row = cases // piece
    packed = s2.shape[1] - piece < piece
    half = LANES // 2

    for i in range(chunks):
        part = pl.ds(i * rows_c, rows_c)
        pltpu.make_async_copy(basis_h.at[part], basis.at[part], bsem.at[i]).start()
    flex_copy = pltpu.make_async_copy(flex_h, flex, bsem.at[chunks])
    flex_copy.start()

    barrier = pltpu.get_barrier_semaphore()

    def greet(k, c):
        pl.semaphore_signal(barrier, inc=1, device_id={"rows": lax.rem(me + k, n)})
        return c

    lax.fori_loop(1, n, greet, 0)

    def remote(phase, k, src, dst, peer):
        return pltpu.make_async_remote_copy(
            src_ref=src,
            dst_ref=dst,
            send_sem=ssem.at[phase, k],
            recv_sem=rsem.at[phase, k],
            device_id={"rows": peer},
        )

    def each(body):
        def step(i, c):
            k = n // 2 + lax.div(i, 2) * (1 - 2 * lax.rem(i, 2))
            body(k, lax.rem(me + k, n), lax.rem(me + n - k, n))
            return c

        lax.fori_loop(1, n, step, 0)

    def only(cond, body):
        if own == n:
            body()
        else:
            pl.when(cond)(body)

    ids = owner[...]
    rows = row[...]
    row_hi = lax.shift_right_logical(rows, 7)
    row_lo = rows & (LANES - 1)
    step_c = 256
    strict = (
        lax.broadcasted_iota(jnp.int32, (step_c, step_c), 0)
        < lax.broadcasted_iota(jnp.int32, (step_c, step_c), 1)
    ).astype(BF16)
    oh_o = (lax.broadcasted_iota(jnp.int32, (n, slots), 0) == ids).astype(F32)
    carry = jnp.zeros((n, 1), F32)
    for b in range(slots // step_c):
        part = oh_o[:, b * step_c : (b + 1) * step_c]
        before = dot(part.astype(BF16), strict) + carry
        carry = carry + jnp.sum(part, axis=1, keepdims=True)
        rank[:, b * step_c : (b + 1) * step_c] = jnp.sum(
            part * before, axis=0, keepdims=True
        ).astype(jnp.int32)
    oh_p = (lax.broadcasted_iota(jnp.int32, (capp, slots), 0) == rank[...]).astype(F32).astype(BF16)
    tiles = tile_count.shape[1]
    lane_id = lax.broadcasted_iota(jnp.int32, (1, slots), 1)
    spread = lax.div(lax.broadcasted_iota(jnp.int32, (tiles, slots), 1), slots // tiles)
    spread = (spread == lax.broadcasted_iota(jnp.int32, (tiles, slots), 0)).astype(F32).astype(BF16)
    counts = jnp.broadcast_to(tile_count[...].astype(F32), (8, tiles)).astype(BF16)
    counts = dot(counts, spread)[0:1, :]
    live[...] = (lax.rem(lane_id, slots // tiles).astype(F32) < counts).astype(F32)
    inv = 1.0 / clear[...]
    weight = live[...] * inv * inv
    w_hi = weight.astype(BF16).astype(F32)
    parts = (row_hi.astype(F32), row_lo.astype(F32), w_hi, weight - w_hi)
    asked = dot_nt(jnp.concatenate([(oh_o * v).astype(BF16) for v in parts], axis=0), oh_p)
    asked_row = asked[0:n] * float(LANES) + asked[n : 2 * n]
    asked_w = asked[2 * n : 3 * n] + asked[3 * n :]
    for o in range(n):
        qs[o, 0:1] = asked_row[o : o + 1, :]
        qs[o, 1:2] = asked_w[o : o + 1, :]

    def ask_copy(k, peer):
        return remote(2, k, qs.at[peer], rq.at[k], peer)

    pl.semaphore_wait(barrier, n - 1)
    each(lambda k, to, fr: ask_copy(k, to).start())
    rq[0] = qs[me]

    xs[0:cases, :] = (thermal[...].astype(F32) + pressure[...].astype(F32)).astype(BF16)
    pad_ids = lax.broadcasted_iota(jnp.int32, (padm.shape[0], nodes), 0)
    hit = (pad_ids & (half - 1)) == node_pad[...]
    coef = heat_coef[...].astype(F32)
    coef = jnp.concatenate([coef[h : h + 1, :] for h in range(his)], axis=1)
    padm[...] = hit.astype(F32).astype(BF16)
    xs[cases:, :] = jnp.where(hit[:pads_r], coef, 0.0).astype(BF16)
    for i in range(chunks):
        part = pl.ds(i * rows_c, rows_c)
        pltpu.make_async_copy(basis_h.at[part], basis.at[part], bsem.at[i]).wait()
        got = dot(xs[:, i * rows_c : (i + 1) * rows_c], basis[part, :])
        if i == 0:
            acc[...] = got
        else:
            acc[...] += got
    for j in range(own):
        blk, r0 = j // per_row, (j % per_row) * piece
        s1[j] = proj_scale * acc[r0 : r0 + piece, blk * LANES : (blk + 1) * LANES]
        h0 = cases + (j % per_row) * rows_h
        hb[j] = proj_scale * acc[h0 : h0 + rows_h, blk * LANES : (blk + 1) * LANES]

    def first_copy(k, peer):
        return remote(0, k, s1.at[peer], r1.at[k], peer)

    each(lambda k, to, fr: only(to < own, lambda: first_copy(k, to).start()))

    def heat_copy(k, peer):
        return remote(3, k, hb.at[peer], rh.at[k], peer)

    def reduce_first():
        each(lambda k, to, fr: first_copy(k, to).wait_recv())
        g1[me] = s1[me] + functools.reduce(lambda a, b: a + b, [r1[k] for k in range(1, n)])

    only(me < own, reduce_first)

    def share_copy(phase, g, k, peer):
        return remote(phase, k, g.at[me], g.at[me], peer)

    def share_wait(phase, g, k, fr):
        remote(phase, k, g.at[fr], g.at[fr], fr).wait_recv()

    only(me < own, lambda: each(lambda k, to, fr: share_copy(4, g1, k, to).start()))
    each(lambda k, to, fr: only(to < own, lambda: heat_copy(k, to).start()))
    each(lambda k, to, fr: ask_copy(k, to).wait_recv())
    both = jnp.zeros((his, 2 * LANES), F32)
    for k in range(n):
        idx = rq[k, 0:1].astype(jnp.int32)
        wgt = rq[k, 1:2]
        top = wgt.astype(BF16).astype(F32)
        hi_hit = lax.broadcasted_iota(jnp.int32, (his, capp), 0) == lax.shift_right_logical(idx, 7)
        lo_hit = lax.broadcasted_iota(jnp.int32, (LANES, capp), 0) == (idx & (LANES - 1))
        b_w = jnp.concatenate(
            [jnp.where(lo_hit, top, 0.0), jnp.where(lo_hit, wgt - top, 0.0)], axis=0
        ).astype(BF16)
        both = both + dot_nt(hi_hit.astype(F32).astype(BF16), b_w)
    wl[...] = both[:, :LANES] + both[:, LANES:]
    eye = lax.broadcasted_iota(jnp.int32, (cases, cases), 0) == lax.broadcasted_iota(
        jnp.int32, (cases, cases), 1
    )
    speed_c = jnp.sum(jnp.where(eye, speed[...], 0.0), axis=1, keepdims=True)
    each(lambda k, to, fr: only(fr < own, lambda: share_wait(4, g1, k, fr)))

    def gathered(g):
        flat = g[...].reshape(own * piece, LANES)
        return jnp.concatenate(
            [flat[m * cases : (m + 1) * cases] for m in range(modes // LANES)], axis=1
        )

    def solve(forcing):
        return mode_scale[...] * (forcing + dot(forcing.astype(BF16), flex[...]))

    flex_copy.wait()
    resp = solve(gathered(g1)).astype(BF16)

    pad_part = jnp.zeros((cases, padm.shape[0]), F32)
    for i in range(chunks):
        lo, hi = i * rows_c, (i + 1) * rows_c
        field = dot_nt(resp, basis[lo:hi, :])
        w_row = jnp.concatenate(
            [wl[h : h + 1, :] for h in range(lo // LANES, hi // LANES)], axis=1
        )
        press = speed_c * jnp.exp(-2.0 * jnp.tanh(0.25 * field)) * w_row
        press_o[:, lo:hi] = press
        press = press.astype(BF16)
        got = dot(press, basis[lo:hi, :])
        if i == 0:
            acc[0:cases, :] = got
        else:
            acc[0:cases, :] += got
        pad_part = pad_part + dot_nt(press, padm[:, lo:hi])
    low = lax.broadcasted_iota(jnp.int32, (cases, LANES), 1) < half
    for j in range(own):
        blk, r0 = j // per_row, (j % per_row) * piece
        s2[j, 0:piece] = proj_scale * acc[r0 : r0 + piece, blk * LANES : (blk + 1) * LANES]
        if packed:
            mid = r0 + piece // 2
            s2[j, piece:] = jnp.where(low[r0:mid], pad_part[r0:mid], pad_part[mid : r0 + piece])
        else:
            s2[j, piece:] = pad_part[r0 : r0 + piece, :]

    def out_copy(i, src, dst):
        return pltpu.make_async_copy(src, dst, osem.at[i])

    def second_copy(k, peer):
        return remote(5, k, s2.at[peer], r2.at[k], peer)

    each(lambda k, to, fr: only(to < own, lambda: second_copy(k, to).start()))

    out_copy(0, press_o, press_h).start()
    mine_h = lax.rem(me, per_row)

    def mate_copy(d):
        mate = me - mine_h + lax.rem(mine_h + d, per_row)
        return pltpu.make_async_remote_copy(
            src_ref=hfull.at[mine_h],
            dst_ref=hfull.at[mine_h],
            send_sem=ssem.at[1, d],
            recv_sem=rsem.at[1, d],
            device_id={"rows": mate},
        )

    def mate_wait(d):
        other = lax.rem(mine_h + per_row - d, per_row)
        pltpu.make_async_remote_copy(
            src_ref=hfull.at[other],
            dst_ref=hfull.at[other],
            send_sem=ssem.at[1, d],
            recv_sem=rsem.at[1, d],
            device_id={"rows": me - mine_h + other},
        ).wait_recv()

    def reduce_second():
        each(lambda k, to, fr: heat_copy(k, to).wait_recv())
        hfull[mine_h] = hb[me] + functools.reduce(
            lambda a, b: a + b, [rh[k] for k in range(1, n)]
        )
        for d in range(1, per_row):
            mate_copy(d).start()
        fac = jnp.concatenate(
            [pad_factor[...], jnp.zeros((1, half - pad_factor.shape[1]), F32)], axis=1
        )
        fac = jnp.concatenate([fac, fac], axis=1) * (pad_factor.shape[1] / (LIVE_DEV * n))
        for d in range(1, per_row):
            mate_wait(d)
        heat = hfull[...].reshape(pads_r, LANES)
        if pads_r < half:
            heat = jnp.concatenate([heat, jnp.zeros((half - pads_r, LANES), F32)], axis=0)
        heat = jnp.concatenate([heat, heat], axis=0)
        each(lambda k, to, fr: second_copy(k, to).wait_recv())
        total = s2[me] + functools.reduce(lambda a, b: a + b, [r2[k] for k in range(1, n)])
        pad_heat = total[piece:] * fac
        left = low[: pad_heat.shape[0]]
        rows_l = jnp.where(left, pad_heat, 0.0)
        if packed:
            rows_l = jnp.concatenate([rows_l, jnp.where(left, 0.0, pad_heat)], axis=0)
        g2[me] = (
            g1[me]
            + total[:piece]
            + jnp.dot(rows_l, heat, precision=lax.Precision.HIGHEST, preferred_element_type=F32)
        )

    only(me < own, reduce_second)
    only(me < own, lambda: each(lambda k, to, fr: share_copy(6, g2, k, to).start()))
    each(lambda k, to, fr: only(fr < own, lambda: share_wait(6, g2, k, fr)))
    resp2 = solve(gathered(g2))
    resp_o[...] = resp2
    out_copy(1, resp_o, resp_h).start()
    resp2 = resp2.astype(BF16)
    for i in range(chunks):
        lo, hi = i * rows_c, (i + 1) * rows_c
        defl_o[:, lo:hi] = dot_nt(resp2, basis[lo:hi, :])

    out_copy(2, defl_o, defl_h).start()


    def pick(k):
        out = []
        for c in range(capp // LANES):
            idx = jnp.broadcast_to(rq[k, 0:1, c * LANES : (c + 1) * LANES].astype(jnp.int32), (cases, LANES))
            idx_hi = lax.shift_right_logical(idx, 7)
            idx_lo = idx & (LANES - 1)
            val = jnp.zeros((cases, LANES), F32)
            for h in range(his):
                got = jnp.take_along_axis(defl_o[:, h * LANES : (h + 1) * LANES], idx_lo, axis=1)
                val = jnp.where(idx_hi == h, got, val)
            out.append(val)
        return jnp.concatenate(out, axis=1) if len(out) > 1 else out[0]

    def answer_copy(k, peer):
        return remote(7, k, fs.at[k], rf.at[me], peer)

    def answer(k, to, fr):
        fs[k] = pick(k)
        answer_copy(k, fr).start()

    each(answer)
    rf[me] = pick(0)
    each(lambda k, to, fr: remote(7, k, fs.at[k], rf.at[to], to).wait_recv())

    def place(t, c):
        part = pl.ds(pl.multiple_of(t * LANES, LANES), LANES)
        own_t = jnp.broadcast_to(owner[:, part], (cases, LANES))
        pos_t = jnp.broadcast_to(rank[:, part], (cases, LANES))
        blk = own_t * (capp // LANES) + lax.shift_right_logical(pos_t, 7)
        lane = pos_t & (LANES - 1)
        val = jnp.zeros((cases, LANES), F32)
        for o in range(n):
            for s in range(capp // LANES):
                got = jnp.take_along_axis(rf[o, :, s * LANES : (s + 1) * LANES], lane, axis=1)
                val = jnp.where(blk == o * (capp // LANES) + s, got, val)
        gap_o[:, part] = live[:, part] * clear[:, part] * jnp.exp(jnp.tanh(0.25 * val))
        return c

    lax.fori_loop(0, slots // LANES, place, 0)
    out_copy(3, gap_o, gap_h).start()

    def drain(k, to, fr):
        def owned():
            first_copy(k, to).wait_send()
            heat_copy(k, to).wait_send()
            second_copy(k, to).wait_send()

        def mine():
            share_copy(4, g1, k, to).wait_send()
            share_copy(6, g2, k, to).wait_send()

        ask_copy(k, to).wait_send()
        answer_copy(k, fr).wait_send()
        only(to < own, owned)
        only(me < own, mine)

    each(drain)
    for d in range(1, per_row):
        only(me < own, lambda: mate_copy(d).wait_send())
    out_copy(0, press_o, press_h).wait()
    out_copy(1, resp_o, resp_h).wait()
    out_copy(2, defl_o, defl_h).wait()
    out_copy(3, gap_o, gap_h).wait()


def hand_over(*refs):
    count = (len(refs) - 1) // 3
    sems = refs[-1]
    ins, outs, held = (refs[i * count : (i + 1) * count] for i in range(3))
    order = (3, 1, 0, 2)
    first = [pltpu.make_async_copy(ins[i], held[i], sems.at[0, i]) for i in order]
    second = [pltpu.make_async_copy(held[i], outs[i], sems.at[1, i]) for i in order]
    for c in first:
        c.start()
    for c, d in zip(first, second):
        c.wait()
        d.start()
    for d in second:
        d.wait()


def on_device(
    basis,
    thermal_load,
    pressure_load,
    heat_coef,
    node_pad,
    pad_factor,
    node_owner,
    node_row,
    tile_count,
    clearance,
    speed,
    mode_scale,
    modal_flex,
):
    n = lax.axis_size("rows")
    nodes, modes = basis.shape
    cases = thermal_load.shape[0]
    slots = node_row.shape[0]
    capacity = 2 * slots // n
    capp = max(LANES, -(-capacity // LANES) * LANES)
    tiles = tile_count.shape[1]
    tile_pts = slots // tiles
    pads = pad_factor.shape[0]
    all_tiles = cases * modes // LANES
    own = min(n, all_tiles // 8)
    piece = all_tiles // own
    per_row = cases // piece
    rows_h = -(-pads // (8 * per_row)) * 8
    pads_r = rows_h * per_row
    extra = piece // 2 if piece % 16 == 0 else piece
    his = nodes // LANES
    chunks = 8

    vmem = pl.BlockSpec(memory_space=pltpu.VMEM)
    anyw = pl.BlockSpec(memory_space=pl.ANY)
    outs = pl.pallas_call(
        functools.partial(kernel, n, own),
        out_shape=(
            jax.ShapeDtypeStruct((cases, nodes), F32),
            jax.ShapeDtypeStruct((cases, modes), F32),
            jax.ShapeDtypeStruct((cases, slots), F32),
            jax.ShapeDtypeStruct((cases, nodes), F32),
        ),
        in_specs=[anyw] + [vmem] * 11 + [anyw],
        out_specs=(anyw,) * 4,
        scratch_shapes=[
            pltpu.VMEM((cases, nodes), F32),
            pltpu.VMEM((cases, modes), F32),
            pltpu.VMEM((cases, slots), F32),
            pltpu.VMEM((cases, nodes), F32),
            pltpu.VMEM((nodes, modes), BF16),
            pltpu.VMEM((modes, modes), BF16),
            pltpu.VMEM((cases + pads_r, nodes), BF16),
            pltpu.VMEM((LANES, nodes), BF16),
            pltpu.VMEM((1, slots), F32),
            pltpu.VMEM((his, LANES), F32),
            pltpu.VMEM((n, 2, capp), F32),
            pltpu.VMEM((n, 2, capp), F32),
            pltpu.VMEM((1, slots), jnp.int32),
            pltpu.VMEM((own, piece, LANES), F32),
            pltpu.VMEM((n, piece, LANES), F32),
            pltpu.VMEM((own, piece, LANES), F32),
            pltpu.VMEM((own, rows_h, LANES), F32),
            pltpu.VMEM((n, rows_h, LANES), F32),
            pltpu.VMEM((per_row, rows_h, LANES), F32),
            pltpu.VMEM((own, piece + extra, LANES), F32),
            pltpu.VMEM((n, piece + extra, LANES), F32),
            pltpu.VMEM((own, piece, LANES), F32),
            pltpu.VMEM((n, cases, capp), F32),
            pltpu.VMEM((n, cases, capp), F32),
            pltpu.VMEM((cases + pads_r, modes), F32),
            pltpu.SemaphoreType.DMA((chunks + 1,)),
            pltpu.SemaphoreType.DMA((4,)),
            pltpu.SemaphoreType.DMA((8, n)),
            pltpu.SemaphoreType.DMA((8, n)),
        ],
        compiler_params=pltpu.CompilerParams(
            collective_id=0, has_side_effects=True, vmem_limit_bytes=56 * 1024 * 1024
        ),
    )(
        basis,
        thermal_load,
        pressure_load,
        heat_coef.reshape(his, LANES),
        node_pad.reshape(1, nodes),
        pad_factor.reshape(1, pads),
        node_owner.reshape(1, slots),
        node_row.reshape(1, slots),
        tile_count,
        clearance.reshape(1, slots),
        speed.reshape(1, cases),
        mode_scale.reshape(1, modes),
        modal_flex,
    )
    return pl.pallas_call(
        hand_over,
        out_shape=tuple(jax.ShapeDtypeStruct(o.shape, o.dtype) for o in outs),
        in_specs=[anyw] * 4,
        out_specs=(anyw,) * 4,
        scratch_shapes=[pltpu.VMEM(o.shape, o.dtype) for o in outs] + [pltpu.SemaphoreType.DMA((2, 4))],
        compiler_params=pltpu.CompilerParams(vmem_limit_bytes=60 * 1024 * 1024),
    )(*outs)


def solution(mesh):
    return jax.shard_map(
        on_device,
        mesh=mesh,
        in_specs=(
            P(("group", "rows"), None),
            P(None, ("group", "rows")),
            P(None, ("group", "rows")),
            P(("group", "rows")),
            P(("group", "rows")),
            P("group"),
            P(("group", "rows"), None),
            P(("group", "rows")),
            P(("group", "rows"), None),
            P(("group", "rows")),
            P(),
            P("group"),
            P("group", None),
        ),
        out_specs=(
            P(None, ("group", "rows")),
            P("group", None),
            P(None, ("group", "rows")),
            P(None, ("group", "rows")),
        ),
        check_vma=False,
    )
```

```python
import functools
import math

import jax
import jax.numpy as jnp
from jax import lax
from jax.experimental import pallas as pl
from jax.experimental.pallas import tpu as pltpu
from jax.sharding import PartitionSpec as P

LIVE_DEV = 1792
LANES = 128
F32 = jnp.float32
BF16 = jnp.bfloat16
NT = (((1,), (1,)), ((), ()))


def dot(a, b):
    return jnp.dot(a, b, preferred_element_type=F32)


def dot_nt(a, b):
    return lax.dot_general(a, b, NT, preferred_element_type=F32)


def kernel(
    n,
    own,
    basis_h,
    thermal,
    pressure,
    heat_coef,
    node_pad,
    pad_factor,
    owner,
    row,
    tile_count,
    clear,
    speed,
    mode_scale,
    flex_h,
    defl_h,
    resp_h,
    gap_h,
    press_h,
    defl_o,
    resp_o,
    gap_o,
    press_o,
    basis,
    flex,
    xs,
    padm,
    live,
    wl,
    qs,
    rq,
    rank,
    s1,
    r1,
    g1,
    hb,
    rh,
    hfull,
    s2,
    r2,
    g2,
    fs,
    rf,
    acc,
    bsem,
    osem,
    ssem,
    rsem,
):
    me = lax.axis_index("rows")
    cases, modes = resp_o.shape
    nodes = basis.shape[0]
    slots = row.shape[1]
    rows_h = rh.shape[1]
    pads_r = xs.shape[0] - cases
    piece = s1.shape[1]
    capp = rq.shape[2]
    his = nodes // LANES
    chunks = bsem.shape[0] - 1
    rows_c = nodes // chunks
    proj_scale = math.sqrt(modes / (nodes * n))
    per_row = cases // piece
    packed = s2.shape[1] - piece < piece
    half = LANES // 2

    for i in range(chunks):
        part = pl.ds(i * rows_c, rows_c)
        pltpu.make_async_copy(basis_h.at[part], basis.at[part], bsem.at[i]).start()
    flex_copy = pltpu.make_async_copy(flex_h, flex, bsem.at[chunks])
    flex_copy.start()

    barrier = pltpu.get_barrier_semaphore()

    def greet(k, c):
        pl.semaphore_signal(barrier, inc=1, device_id={"rows": lax.rem(me + k, n)})
        return c

    lax.fori_loop(1, n, greet, 0)

    def remote(phase, k, src, dst, peer):
        return pltpu.make_async_remote_copy(
            src_ref=src,
            dst_ref=dst,
            send_sem=ssem.at[phase, k],
            recv_sem=rsem.at[phase, k],
            device_id={"rows": peer},
        )

    def each(body):
        def step(i, c):
            k = n // 2 + lax.div(i, 2) * (1 - 2 * lax.rem(i, 2))
            body(k, lax.rem(me + k, n), lax.rem(me + n - k, n))
            return c

        lax.fori_loop(1, n, step, 0)

    def only(cond, body):
        if own == n:
            body()
        else:
            pl.when(cond)(body)

    ids = owner[...]
    rows = row[...]
    row_hi = lax.shift_right_logical(rows, 7)
    row_lo = rows & (LANES - 1)
    step_c = 256
    strict = (
        lax.broadcasted_iota(jnp.int32, (step_c, step_c), 0)
        < lax.broadcasted_iota(jnp.int32, (step_c, step_c), 1)
    ).astype(BF16)
    oh_o = (lax.broadcasted_iota(jnp.int32, (n, slots), 0) == ids).astype(F32)
    carry = jnp.zeros((n, 1), F32)
    for b in range(slots // step_c):
        part = oh_o[:, b * step_c : (b + 1) * step_c]
        before = dot(part.astype(BF16), strict) + carry
        carry = carry + jnp.sum(part, axis=1, keepdims=True)
        rank[:, b * step_c : (b + 1) * step_c] = jnp.sum(
            part * before, axis=0, keepdims=True
        ).astype(jnp.int32)
    oh_p = (lax.broadcasted_iota(jnp.int32, (capp, slots), 0) == rank[...]).astype(F32).astype(BF16)
    tiles = tile_count.shape[1]
    lane_id = lax.broadcasted_iota(jnp.int32, (1, slots), 1)
    spread = lax.div(lax.broadcasted_iota(jnp.int32, (tiles, slots), 1), slots // tiles)
    spread = (spread == lax.broadcasted_iota(jnp.int32, (tiles, slots), 0)).astype(F32).astype(BF16)
    counts = jnp.broadcast_to(tile_count[...].astype(F32), (8, tiles)).astype(BF16)
    counts = dot(counts, spread)[0:1, :]
    live[...] = (lax.rem(lane_id, slots // tiles).astype(F32) < counts).astype(F32)
    inv = 1.0 / clear[...]
    weight = live[...] * inv * inv
    w_hi = weight.astype(BF16).astype(F32)
    parts = (row_hi.astype(F32), row_lo.astype(F32), w_hi, weight - w_hi)
    asked = dot_nt(jnp.concatenate([(oh_o * v).astype(BF16) for v in parts], axis=0), oh_p)
    asked_row = asked[0:n] * float(LANES) + asked[n : 2 * n]
    asked_w = asked[2 * n : 3 * n] + asked[3 * n :]
    for o in range(n):
        qs[o, 0:1] = asked_row[o : o + 1, :]
        qs[o, 1:2] = asked_w[o : o + 1, :]

    def ask_copy(k, peer):
        return remote(2, k, qs.at[peer], rq.at[k], peer)

    pl.semaphore_wait(barrier, n - 1)
    each(lambda k, to, fr: ask_copy(k, to).start())
    rq[0] = qs[me]

    xs[0:cases, :] = (thermal[...].astype(F32) + pressure[...].astype(F32)).astype(BF16)
    pad_ids = lax.broadcasted_iota(jnp.int32, (padm.shape[0], nodes), 0)
    hit = (pad_ids & (half - 1)) == node_pad[...]
    coef = heat_coef[...].astype(F32)
    coef = jnp.concatenate([coef[h : h + 1, :] for h in range(his)], axis=1)
    padm[...] = hit.astype(F32).astype(BF16)
    xs[cases:, :] = jnp.where(hit[:pads_r], coef, 0.0).astype(BF16)
    for i in range(chunks):
        part = pl.ds(i * rows_c, rows_c)
        pltpu.make_async_copy(basis_h.at[part], basis.at[part], bsem.at[i]).wait()
        got = dot(xs[:, i * rows_c : (i + 1) * rows_c], basis[part, :])
        if i == 0:
            acc[...] = got
        else:
            acc[...] += got
    for j in range(own):
        blk, r0 = j // per_row, (j % per_row) * piece
        s1[j] = proj_scale * acc[r0 : r0 + piece, blk * LANES : (blk + 1) * LANES]
        h0 = cases + (j % per_row) * rows_h
        hb[j] = proj_scale * acc[h0 : h0 + rows_h, blk * LANES : (blk + 1) * LANES]

    def first_copy(k, peer):
        return remote(0, k, s1.at[peer], r1.at[k], peer)

    each(lambda k, to, fr: only(to < own, lambda: first_copy(k, to).start()))

    def heat_copy(k, peer):
        return remote(3, k, hb.at[peer], rh.at[k], peer)

    def reduce_first():
        each(lambda k, to, fr: first_copy(k, to).wait_recv())
        g1[me] = s1[me] + functools.reduce(lambda a, b: a + b, [r1[k] for k in range(1, n)])

    only(me < own, reduce_first)

    def share_copy(phase, g, k, peer):
        return remote(phase, k, g.at[me], g.at[me], peer)

    def share_wait(phase, g, k, fr):
        remote(phase, k, g.at[fr], g.at[fr], fr).wait_recv()

    only(me < own, lambda: each(lambda k, to, fr: share_copy(4, g1, k, to).start()))
    each(lambda k, to, fr: ask_copy(k, to).wait_recv())
    both = jnp.zeros((his, 2 * LANES), F32)
    for k in range(n):
        idx = rq[k, 0:1].astype(jnp.int32)
        wgt = rq[k, 1:2]
        top = wgt.astype(BF16).astype(F32)
        hi_hit = lax.broadcasted_iota(jnp.int32, (his, capp), 0) == lax.shift_right_logical(idx, 7)
        lo_hit = lax.broadcasted_iota(jnp.int32, (LANES, capp), 0) == (idx & (LANES - 1))
        b_w = jnp.concatenate(
            [jnp.where(lo_hit, top, 0.0), jnp.where(lo_hit, wgt - top, 0.0)], axis=0
        ).astype(BF16)
        both = both + dot_nt(hi_hit.astype(F32).astype(BF16), b_w)
    wl[...] = both[:, :LANES] + both[:, LANES:]
    eye = lax.broadcasted_iota(jnp.int32, (cases, cases), 0) == lax.broadcasted_iota(
        jnp.int32, (cases, cases), 1
    )
    speed_c = jnp.sum(jnp.where(eye, speed[...], 0.0), axis=1, keepdims=True)
    each(lambda k, to, fr: only(fr < own, lambda: share_wait(4, g1, k, fr)))
    each(lambda k, to, fr: only(to < own, lambda: heat_copy(k, to).start()))

    def gathered(g):
        flat = g[...].reshape(own * piece, LANES)
        return jnp.concatenate(
            [flat[m * cases : (m + 1) * cases] for m in range(modes // LANES)], axis=1
        )

    def solve(forcing):
        return mode_scale[...] * (forcing + dot(forcing.astype(BF16), flex[...]))

    flex_copy.wait()
    resp = solve(gathered(g1)).astype(BF16)

    pad_part = jnp.zeros((cases, padm.shape[0]), F32)
    for i in range(chunks):
        lo, hi = i * rows_c, (i + 1) * rows_c
        field = dot_nt(resp, basis[lo:hi, :])
        w_row = jnp.concatenate(
            [wl[h : h + 1, :] for h in range(lo // LANES, hi // LANES)], axis=1
        )
        press = speed_c * jnp.exp(-2.0 * jnp.tanh(0.25 * field)) * w_row
        press_o[:, lo:hi] = press
        press = press.astype(BF16)
        got = dot(press, basis[lo:hi, :])
        if i == 0:
            acc[0:cases, :] = got
        else:
            acc[0:cases, :] += got
        pad_part = pad_part + dot_nt(press, padm[:, lo:hi])
    low = lax.broadcasted_iota(jnp.int32, (cases, LANES), 1) < half
    for j in range(own):
        blk, r0 = j // per_row, (j % per_row) * piece
        s2[j, 0:piece] = proj_scale * acc[r0 : r0 + piece, blk * LANES : (blk + 1) * LANES]
        if packed:
            mid = r0 + piece // 2
            s2[j, piece:] = jnp.where(low[r0:mid], pad_part[r0:mid], pad_part[mid : r0 + piece])
        else:
            s2[j, piece:] = pad_part[r0 : r0 + piece, :]

    def out_copy(i, src, dst):
        return pltpu.make_async_copy(src, dst, osem.at[i])

    def second_copy(k, peer):
        return remote(5, k, s2.at[peer], r2.at[k], peer)

    each(lambda k, to, fr: only(to < own, lambda: second_copy(k, to).start()))

    out_copy(0, press_o, press_h).start()
    mine_h = lax.rem(me, per_row)

    def mate_copy(d):
        mate = me - mine_h + lax.rem(mine_h + d, per_row)
        return pltpu.make_async_remote_copy(
            src_ref=hfull.at[mine_h],
            dst_ref=hfull.at[mine_h],
            send_sem=ssem.at[1, d],
            recv_sem=rsem.at[1, d],
            device_id={"rows": mate},
        )

    def mate_wait(d):
        other = lax.rem(mine_h + per_row - d, per_row)
        pltpu.make_async_remote_copy(
            src_ref=hfull.at[other],
            dst_ref=hfull.at[other],
            send_sem=ssem.at[1, d],
            recv_sem=rsem.at[1, d],
            device_id={"rows": me - mine_h + other},
        ).wait_recv()

    def reduce_second():
        each(lambda k, to, fr: heat_copy(k, to).wait_recv())
        hfull[mine_h] = hb[me] + functools.reduce(
            lambda a, b: a + b, [rh[k] for k in range(1, n)]
        )
        for d in range(1, per_row):
            mate_copy(d).start()
        fac = jnp.concatenate(
            [pad_factor[...], jnp.zeros((1, half - pad_factor.shape[1]), F32)], axis=1
        )
        fac = jnp.concatenate([fac, fac], axis=1) * (pad_factor.shape[1] / (LIVE_DEV * n))
        for d in range(1, per_row):
            mate_wait(d)
        heat = hfull[...].reshape(pads_r, LANES)
        if pads_r < half:
            heat = jnp.concatenate([heat, jnp.zeros((half - pads_r, LANES), F32)], axis=0)
        heat = jnp.concatenate([heat, heat], axis=0)
        each(lambda k, to, fr: second_copy(k, to).wait_recv())
        total = s2[me] + functools.reduce(lambda a, b: a + b, [r2[k] for k in range(1, n)])
        pad_heat = total[piece:] * fac
        left = low[: pad_heat.shape[0]]
        rows_l = jnp.where(left, pad_heat, 0.0)
        if packed:
            rows_l = jnp.concatenate([rows_l, jnp.where(left, 0.0, pad_heat)], axis=0)
        g2[me] = (
            g1[me]
            + total[:piece]
            + jnp.dot(rows_l, heat, precision=lax.Precision.HIGHEST, preferred_element_type=F32)
        )

    only(me < own, reduce_second)
    only(me < own, lambda: each(lambda k, to, fr: share_copy(6, g2, k, to).start()))
    each(lambda k, to, fr: only(fr < own, lambda: share_wait(6, g2, k, fr)))
    resp2 = solve(gathered(g2))
    resp_o[...] = resp2
    out_copy(1, resp_o, resp_h).start()
    resp2 = resp2.astype(BF16)
    for i in range(chunks):
        lo, hi = i * rows_c, (i + 1) * rows_c
        defl_o[:, lo:hi] = dot_nt(resp2, basis[lo:hi, :])

    out_copy(2, defl_o, defl_h).start()


    def pick(k):
        out = []
        for c in range(capp // LANES):
            idx = jnp.broadcast_to(rq[k, 0:1, c * LANES : (c + 1) * LANES].astype(jnp.int32), (cases, LANES))
            idx_hi = lax.shift_right_logical(idx, 7)
            idx_lo = idx & (LANES - 1)
            val = jnp.zeros((cases, LANES), F32)
            for h in range(his):
                got = jnp.take_along_axis(defl_o[:, h * LANES : (h + 1) * LANES], idx_lo, axis=1)
                val = jnp.where(idx_hi == h, got, val)
            out.append(val)
        return jnp.concatenate(out, axis=1) if len(out) > 1 else out[0]

    def answer_copy(k, peer):
        return remote(7, k, fs.at[k], rf.at[me], peer)

    def answer(k, to, fr):
        fs[k] = pick(k)
        answer_copy(k, fr).start()

    each(answer)
    rf[me] = pick(0)
    each(lambda k, to, fr: remote(7, k, fs.at[k], rf.at[to], to).wait_recv())

    def place(t, c):
        part = pl.ds(pl.multiple_of(t * LANES, LANES), LANES)
        own_t = jnp.broadcast_to(owner[:, part], (cases, LANES))
        pos_t = jnp.broadcast_to(rank[:, part], (cases, LANES))
        blk = own_t * (capp // LANES) + lax.shift_right_logical(pos_t, 7)
        lane = pos_t & (LANES - 1)
        val = jnp.zeros((cases, LANES), F32)
        for o in range(n):
            for s in range(capp // LANES):
                got = jnp.take_along_axis(rf[o, :, s * LANES : (s + 1) * LANES], lane, axis=1)
                val = jnp.where(blk == o * (capp // LANES) + s, got, val)
        gap_o[:, part] = live[:, part] * clear[:, part] * jnp.exp(jnp.tanh(0.25 * val))
        return c

    lax.fori_loop(0, slots // LANES, place, 0)
    out_copy(3, gap_o, gap_h).start()

    def drain(k, to, fr):
        def owned():
            first_copy(k, to).wait_send()
            heat_copy(k, to).wait_send()
            second_copy(k, to).wait_send()

        def mine():
            share_copy(4, g1, k, to).wait_send()
            share_copy(6, g2, k, to).wait_send()

        ask_copy(k, to).wait_send()
        answer_copy(k, fr).wait_send()
        only(to < own, owned)
        only(me < own, mine)

    each(drain)
    for d in range(1, per_row):
        only(me < own, lambda: mate_copy(d).wait_send())
    out_copy(0, press_o, press_h).wait()
    out_copy(1, resp_o, resp_h).wait()
    out_copy(2, defl_o, defl_h).wait()
    out_copy(3, gap_o, gap_h).wait()


def hand_over(*refs):
    count = (len(refs) - 1) // 3
    sems = refs[-1]
    ins, outs, held = (refs[i * count : (i + 1) * count] for i in range(3))
    order = (3, 1, 0, 2)
    first = [pltpu.make_async_copy(ins[i], held[i], sems.at[0, i]) for i in order]
    second = [pltpu.make_async_copy(held[i], outs[i], sems.at[1, i]) for i in order]
    for c in first:
        c.start()
    for c, d in zip(first, second):
        c.wait()
        d.start()
    for d in second:
        d.wait()


def on_device(
    basis,
    thermal_load,
    pressure_load,
    heat_coef,
    node_pad,
    pad_factor,
    node_owner,
    node_row,
    tile_count,
    clearance,
    speed,
    mode_scale,
    modal_flex,
):
    n = lax.axis_size("rows")
    nodes, modes = basis.shape
    cases = thermal_load.shape[0]
    slots = node_row.shape[0]
    capacity = 2 * slots // n
    capp = max(LANES, -(-capacity // LANES) * LANES)
    tiles = tile_count.shape[1]
    tile_pts = slots // tiles
    pads = pad_factor.shape[0]
    all_tiles = cases * modes // LANES
    own = min(n, all_tiles // 8)
    piece = all_tiles // own
    per_row = cases // piece
    rows_h = -(-pads // (8 * per_row)) * 8
    pads_r = rows_h * per_row
    extra = piece // 2 if piece % 16 == 0 else piece
    his = nodes // LANES
    chunks = 8

    vmem = pl.BlockSpec(memory_space=pltpu.VMEM)
    anyw = pl.BlockSpec(memory_space=pl.ANY)
    outs = pl.pallas_call(
        functools.partial(kernel, n, own),
        out_shape=(
            jax.ShapeDtypeStruct((cases, nodes), F32),
            jax.ShapeDtypeStruct((cases, modes), F32),
            jax.ShapeDtypeStruct((cases, slots), F32),
            jax.ShapeDtypeStruct((cases, nodes), F32),
        ),
        in_specs=[anyw] + [vmem] * 11 + [anyw],
        out_specs=(anyw,) * 4,
        scratch_shapes=[
            pltpu.VMEM((cases, nodes), F32),
            pltpu.VMEM((cases, modes), F32),
            pltpu.VMEM((cases, slots), F32),
            pltpu.VMEM((cases, nodes), F32),
            pltpu.VMEM((nodes, modes), BF16),
            pltpu.VMEM((modes, modes), BF16),
            pltpu.VMEM((cases + pads_r, nodes), BF16),
            pltpu.VMEM((LANES, nodes), BF16),
            pltpu.VMEM((1, slots), F32),
            pltpu.VMEM((his, LANES), F32),
            pltpu.VMEM((n, 2, capp), F32),
            pltpu.VMEM((n, 2, capp), F32),
            pltpu.VMEM((1, slots), jnp.int32),
            pltpu.VMEM((own, piece, LANES), F32),
            pltpu.VMEM((n, piece, LANES), F32),
            pltpu.VMEM((own, piece, LANES), F32),
            pltpu.VMEM((own, rows_h, LANES), F32),
            pltpu.VMEM((n, rows_h, LANES), F32),
            pltpu.VMEM((per_row, rows_h, LANES), F32),
            pltpu.VMEM((own, piece + extra, LANES), F32),
            pltpu.VMEM((n, piece + extra, LANES), F32),
            pltpu.VMEM((own, piece, LANES), F32),
            pltpu.VMEM((n, cases, capp), F32),
            pltpu.VMEM((n, cases, capp), F32),
            pltpu.VMEM((cases + pads_r, modes), F32),
            pltpu.SemaphoreType.DMA((chunks + 1,)),
            pltpu.SemaphoreType.DMA((4,)),
            pltpu.SemaphoreType.DMA((8, n)),
            pltpu.SemaphoreType.DMA((8, n)),
        ],
        compiler_params=pltpu.CompilerParams(
            collective_id=0, has_side_effects=True, vmem_limit_bytes=56 * 1024 * 1024
        ),
    )(
        basis,
        thermal_load,
        pressure_load,
        heat_coef.reshape(his, LANES),
        node_pad.reshape(1, nodes),
        pad_factor.reshape(1, pads),
        node_owner.reshape(1, slots),
        node_row.reshape(1, slots),
        tile_count,
        clearance.reshape(1, slots),
        speed.reshape(1, cases),
        mode_scale.reshape(1, modes),
        modal_flex,
    )
    return pl.pallas_call(
        hand_over,
        out_shape=tuple(jax.ShapeDtypeStruct(o.shape, o.dtype) for o in outs),
        in_specs=[anyw] * 4,
        out_specs=(anyw,) * 4,
        scratch_shapes=[pltpu.VMEM(o.shape, o.dtype) for o in outs] + [pltpu.SemaphoreType.DMA((2, 4))],
        compiler_params=pltpu.CompilerParams(vmem_limit_bytes=60 * 1024 * 1024),
    )(*outs)


def solution(mesh):
    return jax.shard_map(
        on_device,
        mesh=mesh,
        in_specs=(
            P(("group", "rows"), None),
            P(None, ("group", "rows")),
            P(None, ("group", "rows")),
            P(("group", "rows")),
            P(("group", "rows")),
            P("group"),
            P(("group", "rows"), None),
            P(("group", "rows")),
            P(("group", "rows"), None),
            P(("group", "rows")),
            P(),
            P("group"),
            P("group", None),
        ),
        out_specs=(
            P(None, ("group", "rows")),
            P("group", None),
            P(None, ("group", "rows")),
            P(None, ("group", "rows")),
        ),
        check_vma=False,
    )
```
